128 devices in a mesh: ex: 32 (over x, y, core), layer: 4 (over z).
Axes of the slice: x: 4, y: 4, z: 4, core: 2. Of those that a mesh axis runs over, the one named last changes fastest.
Arguments:
- store: bfloat16 [131072, 8192], P('ex', 'layer'), as said below
- precond: bfloat16 [4, 2048, 2048], P('layer', 'ex'), as said below
- query_slots: bfloat16 [32, 2, 64, 8192], P('ex', None, None, 'layer'), may hold values from -6 to 6
- owners: int32 [2], replicated, may hold values from 0 to 31
Outputs:
- scores: float32 [131072, 128], P('ex', 'layer')
The draws below stay inside these ranges and needn't reach their ends.
Inputs may be any that keep to these rules, and one draw needn't show every extreme that they name: `store`: training gradients with varying example and entry scales. `precond`: a dense preconditioner for each layer block.
All inputs are finite; a program needn't handle non-finite values.
Results may differ from the reference program's by a relative error of at most 0.0029.
Values may be sent and summed in bfloat16 or wider, within the bound.
No kernel may reach another device: no remote copies, remote signals or barrier semaphores. Data moves between devices by JAX's collectives and lax.ppermute only.
A program may use at most 128 MiB of HBM per device.

```python
import math
import jax
import jax.numpy as jnp
from jax import lax

B = 2048
EX_DEV = 4096
QROWS = 64
QBLOCKS = 2
BLOCKS = 4
FEAT = 8192
QUERIES = 128
SLOTS = 32
EXAMPLES = 131072
N_EX = 32


def draw_store(key, part):
    key = jax.random.fold_in(key, 11)
    key_row, key_col, key_base = jax.random.split(key, 3)
    row_scale = jnp.exp(jax.random.uniform(key_row, (EXAMPLES, 1), jnp.float32) * math.log(10.0))
    col_scale = jnp.exp(jax.random.uniform(key_col, (1, FEAT), jnp.float32) * math.log(10.0))
    block_of = (jnp.arange(FEAT) // B).astype(jnp.float32)
    ramp = jnp.exp(block_of / (BLOCKS - 1) * math.log(3.0))[None, :]
    base = jax.random.normal(key_base, (EXAMPLES, FEAT), jnp.float32)
    return (base * row_scale * col_scale * ramp / 10.0).astype(jnp.bfloat16)


def draw_precond(key, part):
    key = jax.random.fold_in(key, 23)
    key_diag, key_rest = jax.random.split(key)
    diag_vals = jnp.exp(jax.random.uniform(key_diag, (BLOCKS, B, 1), jnp.float32) * math.log(4.0))
    eye = (jnp.arange(B)[:, None] == jnp.arange(B)[None, :]).astype(jnp.float32)
    rest = jax.random.normal(key_rest, (BLOCKS, B, B), jnp.float32) / math.sqrt(B)
    return (diag_vals * eye[None] + rest).astype(jnp.bfloat16)


def levels(rng, extent, cuts, smallest, top_value):
    def one(position, shards_of):
        draws = jax.random.uniform(jax.random.fold_in(jax.random.fold_in(rng, 6), position), (shards_of,), jnp.float32, smallest / len(cuts), top_value / len(cuts))
        return jnp.repeat(jnp.exp(draws), extent[position] // shards_of).reshape((-1,) + (1,) * (len(extent) - position - 1))

    factor_of = one(*cuts[0])
    for cut in cuts[1:]:
        factor_of = factor_of * one(*cut)
    return factor_of


def noise(key, dims, scale, bound, pieces=(), kind=jnp.bfloat16):
    gain = levels(key, dims, pieces, -0.22, 0.18) if pieces else 1.0
    entries = jax.random.normal(key, dims, jnp.float32) * scale * gain
    return jnp.minimum(jnp.maximum(entries, -bound), bound).astype(kind)


def setup_inputs(seed: int = 0) -> dict:
    arg_keys = jax.random.split(jax.random.key(seed), 5)
    return {
        "store": draw_store(jax.random.fold_in(arg_keys[4], 71), 0),
        "precond": draw_precond(jax.random.fold_in(arg_keys[4], 71), 0),
        "query_slots": noise(arg_keys[2], (SLOTS, QBLOCKS, QROWS, FEAT), 1.0, 6.0, ((0, 32), (3, 4))),
        "owners": jax.random.randint(arg_keys[3], (QBLOCKS,), 0, N_EX).astype(jnp.int32),
    }


def reference(store, precond, query_slots, owners):
    picked = [lax.dynamic_index_in_dim(query_slots, owners[b], 0, keepdims=False)[b] for b in range(QBLOCKS)]
    raw = jnp.concatenate(picked, axis=0)
    parts = []
    for block in range(BLOCKS):
        parts.append(jnp.dot(raw[:, block * B:(block + 1) * B], precond[block], preferred_element_type=jnp.float32))
    pre = jnp.concatenate(parts, axis=1).astype(jnp.bfloat16)
    qnorm = lax.optimization_barrier(jnp.sum(jnp.square(pre.astype(jnp.float32)), axis=1))
    stacked = store.reshape(N_EX, EX_DEV, FEAT)

    def one_group(rows):
        gnorm = lax.optimization_barrier(jnp.sum(jnp.square(rows.astype(jnp.float32)), axis=1))
        dots = lax.dot_general(rows, pre, (((1,), (1,)), ((), ())), preferred_element_type=jnp.float32)
        return dots * lax.rsqrt(gnorm + 1e-06)[:, None]
    scaled = lax.map(one_group, stacked).reshape(EXAMPLES, QUERIES)
    factor = jnp.sqrt(jnp.float32(FEAT))
    return scaled * lax.rsqrt(qnorm + 1e-06)[None, :] * factor
```

```python
import functools
import math

import jax
import jax.numpy as jnp
from jax import lax
from jax.experimental import pallas as pl
from jax.experimental.pallas import tpu as pltpu
from jax.sharding import PartitionSpec as P

BF16, F32 = jnp.bfloat16, jnp.float32
NT = (((1,), (1,)), ((), ()))
VMEM = pltpu.VMEM
NX = NY = 4
NZ = 4


def shape(dims, dtype):
    return jax.ShapeDtypeStruct(dims, dtype)


def place():
    e = lax.axis_index("ex")
    return e // 8, (e // 2) % 4, e % 2


def owner_place(owners_ref, block):
    o = owners_ref[block]
    return o // 8, (o // 2) % 4, o % 2


def at(start, size):
    return pl.ds(pl.multiple_of(start, size), size)


def call(body, name, ins, outs, scratch=(), limit=24 << 20, flops=0, moved=1 << 20):
    specs = []
    for a in ins:
        if a.dtype == jnp.int32:
            specs.append(pl.BlockSpec(memory_space=pltpu.SMEM))
        else:
            specs.append(pl.BlockSpec(memory_space=VMEM))
    return pl.pallas_call(
        body,
        name=name,
        in_specs=specs,
        out_specs=[pl.BlockSpec(memory_space=VMEM)] * len(outs),
        out_shape=outs,
        scratch_shapes=scratch,
        compiler_params=pltpu.CompilerParams(vmem_limit_bytes=limit),
        cost_estimate=pl.CostEstimate(flops=flops, bytes_accessed=moved, transcendentals=0),
    )(*ins)


def slices(owners, q, qo, p, po, a0, a1, a2, a3, b0, b1, b2, b3):
    x, y, c = place()
    for block in range(2):
        rows = slice(64 * block, 64 * block + 64)
        mine = owner_place(owners, block)[2] == c
        for d, a in enumerate((a0, a1, a2, a3)):
            columns = at(lax.rem(x + d, 4) * 512, 512)

            @pl.when(mine)
            def _():
                a[rows, :] = q[rows, columns]

            @pl.when(jnp.logical_not(mine))
            def _():
                a[rows, :] = qo[rows, columns]

    for d, b in enumerate((b0, b1, b2, b3)):
        columns = at(c * 1024 + lax.rem(y + d, 4) * 256, 256)
        b[at(c * 64, 64), :] = p[:, columns]
        b[at(64 - c * 64, 64), :] = po[:, columns]


def pack(owners, a0, a1, a2, a3, b1, b2, b3, r, t1, t2, t3):
    x, _, _ = place()
    for block in range(2):
        rows = slice(64 * block, 64 * block + 64)
        back = lax.rem(x - owner_place(owners, block)[0] + 4, 4)
        for d, a in enumerate((a0, a1, a2, a3)):

            @pl.when(back == d)
            def _():
                r[rows, :] = a[rows, :]

    for b, t in ((b1, t1), (b2, t2), (b3, t3)):
        t[:, 0:512] = r[...]
        t[:, 512:768] = b[...]


def product(owners, r, b0, u1, u2, u3, s, raw):
    _, y, _ = place()
    for block in range(2):
        rows = slice(64 * block, 64 * block + 64)
        back = lax.rem(y - owner_place(owners, block)[1] + 4, 4)
        for d, u in enumerate((r, u1, u2, u3)):

            @pl.when(back == d)
            def _():
                raw[rows, :] = u[rows, 0:512]

    total = None
    for d, u in enumerate((b0, u1, u2, u3)):
        piece = u[...] if d == 0 else u[:, 512:768]
        columns = at(lax.rem(y - d + 4, 4) * 128, 128)
        term = jnp.dot(raw[:, columns], piece, preferred_element_type=F32)
        total = term if total is None else total + term
    s[...] = total


def round_sum(s0, s1, s2, s3, w):
    w[...] = ((s0[...] + s2[...]) + (s1[...] + s3[...])).astype(BF16)


def join(w, wo, j):
    _, _, c = place()
    j[:, at(c * 256, 256)] = w[...]
    j[:, at(256 - c * 256, 256)] = wo[...]


ROWS = 512
CHUNKS = 8


def dots(j0, j1, j2, j3, store, own, gn_own, qn_own, z1, z2, z3, pre, half, gn, blocks, sems):
    _, y, _ = place()
    layer = lax.axis_index("layer")
    copies = []
    for i in range(CHUNKS):
        copy = pltpu.make_async_copy(store.at[pl.ds(ROWS * i, ROWS), :], blocks.at[i], sems.at[i])
        copy.start()
        copies.append(copy)
    for d, j in enumerate((j0, j1, j2, j3)):
        origin = lax.rem(y - d + 4, 4) * 256
        for c in range(2):
            pre[:, at(c * 1024 + origin, 256)] = j[:, 256 * c:256 * c + 256]
    q = jnp.square(pre[...].astype(F32))
    qsum = jnp.sum(q, axis=1, keepdims=True)
    qparts = jnp.broadcast_to(qsum, (128, 128))
    gn[...] = qparts
    zs = (None, z1, z2, z3)
    for d in range(4):
        rows = at(lax.rem(layer + d, 4) * 32, 32)
        half[32 * d:32 * d + 32, :] = pre[rows, :] * jnp.asarray(0.5, BF16)
        part = gn[rows, :]
        if d == 0:
            qn_own[...] = part * 0.5
        else:
            part = part * 0.5
            hi = part.astype(BF16)
            lo = (part - hi.astype(F32)).astype(BF16)
            lane = lax.broadcasted_iota(jnp.int32, (32, 128), 1)
            both = jnp.where(lane < 64, hi.astype(F32), lo.astype(F32))
            zs[d][:, 4352:4480] = both.astype(BF16)
    for i in range(CHUNKS):
        copies[i].wait()
        columns = slice(ROWS * i, ROWS * i + ROWS)
        s = blocks[i]
        out = lax.dot_general(s, half[...], NT, preferred_element_type=F32).T
        own[:, columns] = out[0:32, :]
        for d in range(1, 4):
            zs[d][:, columns] = out[32 * d:32 * d + 32, :].astype(BF16)
        squares = None
        for k in range(16):
            v = s[:, 128 * k:128 * k + 128].astype(F32)
            squares = v * v if squares is None else squares + v * v
        line = jnp.sum(squares.T, axis=0, keepdims=True) * 0.5
        for k in range(ROWS // 128):
            row = (ROWS // 128) * i + k
            gn_own[row:row + 1, :] = line[:, 128 * k:128 * k + 128]
    g = gn_own[...]
    hi = g.astype(BF16)
    lo = (g - hi.astype(F32)).astype(BF16)
    for d in range(1, 4):
        zs[d][:, 4096:4224] = hi
        zs[d][:, 4224:4352] = lo


def finish(own, gn_own, qn_own, z1, z2, z3, out):
    g = gn_own[...]
    q = qn_own[:, 0:1]
    for z in (z1, z2, z3):
        g = g + (z[:, 4096:4224].astype(F32) + z[:, 4224:4352].astype(F32))
        q = q + (z[:, 4352:4353].astype(F32) + z[:, 4416:4417].astype(F32))
    g = lax.rsqrt(g * 2.0 + 1e-06)
    q = lax.rsqrt(q * 2.0 + 1e-06) * (2.0 * math.sqrt(8192.0))
    for i in range(32):
        columns = slice(128 * i, 128 * i + 128)
        t = (own[:, columns] + z2[:, columns].astype(F32)) + (
            z1[:, columns].astype(F32) + z3[:, columns].astype(F32)
        )
        out[:, columns] = t * g[i:i + 1, :] * q


def moved(dx, dy, dc):
    pairs = []
    for x in range(4):
        for y in range(4):
            for c in range(2):
                to = ((x + dx) % 4 * 4 + (y + dy) % 4) * 2 + (c + dc) % 2
                pairs.append(((x * 4 + y) * 2 + c, to))
    return pairs


def send(a, dx=0, dy=0, dc=0):
    return lax.ppermute(a, "ex", moved(dx, dy, dc))


def send_layer(a, d):
    return lax.ppermute(a, "layer", [(i, (i + d) % 4) for i in range(4)])


def shards(store, precond, query_slots, owners):
    q = query_slots.reshape(128, 2048)
    p = precond.reshape(64, 2048)
    qo = send(q, dc=1)
    po = send(p, dc=1)
    piece = shape((128, 512), BF16)
    block = shape((128, 256), BF16)
    a0, a1, a2, a3, b0, b1, b2, b3 = call(
        slices, "slices", (owners, q, qo, p, po), [piece] * 4 + [block] * 4
    )
    a1, a2, a3 = send(a1, dx=1), send(a2, dx=2), send(a3, dx=3)
    r, t1, t2, t3 = call(
        pack, "pack", (owners, a0, a1, a2, a3, b1, b2, b3), [piece] + [shape((128, 768), BF16)] * 3
    )
    t1, t2, t3 = send(t1, dy=1), send(t2, dy=2), send(t3, dy=3)
    (s,) = call(
        product, "product", (owners, r, b0, t1, t2, t3), [shape((128, 256), F32)],
        scratch=[VMEM((128, 512), BF16)], flops=2 * 128 * 512 * 256,
    )
    s1, s2, s3 = send(s, dx=1), send(s, dx=2), send(s, dx=3)
    (w,) = call(round_sum, "round_sum", (s, s1, s2, s3), [block])
    wo = send(w, dc=1)
    (j,) = call(join, "join", (w, wo), [piece])
    j1, j2, j3 = send(j, dy=1), send(j, dy=2), send(j, dy=3)
    zshape = shape((32, 4480), BF16)
    vm = pl.BlockSpec(memory_space=VMEM)
    own, gn_own, qn_own, z1, z2, z3 = pl.pallas_call(
        dots,
        name="dots",
        in_specs=[vm] * 4 + [pl.BlockSpec(memory_space=pl.ANY)],
        out_specs=[vm] * 6,
        out_shape=[shape((32, 4096), F32), shape((32, 128), F32), shape((32, 128), F32)] + [zshape] * 3,
        scratch_shapes=[
            VMEM((128, 2048), BF16),
            VMEM((128, 2048), BF16),
            VMEM((128, 128), F32),
            VMEM((CHUNKS, ROWS, 2048), BF16),
            pltpu.SemaphoreType.DMA((CHUNKS,)),
        ],
        compiler_params=pltpu.CompilerParams(vmem_limit_bytes=40 << 20),
        cost_estimate=pl.CostEstimate(flops=2 * 128 * 2048 * 4096, bytes_accessed=17 << 20, transcendentals=0),
    )(j, j1, j2, j3, store)
    z1, z2, z3 = send_layer(z1, 1), send_layer(z2, 2), send_layer(z3, 3)
    (out,) = call(finish, "finish", (own, gn_own, qn_own, z1, z2, z3), [shape((32, 4096), F32)])
    return out.T


def solution(mesh):
    return jax.shard_map(
        shards,
        mesh=mesh,
        in_specs=(P("ex", "layer"), P("layer", "ex", None), P("ex", None, None, "layer"), P()),
        out_specs=P("ex", "layer"),
        check_vma=False,
    )
```

```python
import math

import jax
import jax.numpy as jnp
from jax import lax
from jax.experimental import pallas as pl
from jax.experimental.pallas import tpu as pltpu
from jax.sharding import PartitionSpec as P

BF16, F32 = jnp.bfloat16, jnp.float32
NT = (((1,), (1,)), ((), ()))
VMEM, HBM = pltpu.VMEM, pltpu.HBM
PART = 1024
PARTS = 4


def shape(dims, dtype=BF16):
    return jax.ShapeDtypeStruct(dims, dtype)


def place():
    e = lax.axis_index("ex")
    return e // 8, (e // 2) % 4, e % 2


def at(start, size):
    return pl.ds(pl.multiple_of(start, size), size)


def call(body, name, ins, outs, spaces=None, scratch=(), limit=8 << 20, flops=0, moved=1 << 20, alias=None):
    spaces = spaces or {}
    ins = [pltpu.with_memory_space_constraint(a, HBM) if spaces.get(i) is HBM else a for i, a in enumerate(ins)]
    return pl.pallas_call(
        body,
        name=name,
        in_specs=[pl.BlockSpec(memory_space=spaces.get(i, VMEM)) for i in range(len(ins))],
        out_specs=[pl.BlockSpec(memory_space=VMEM)] * len(outs),
        out_shape=outs,
        scratch_shapes=scratch,
        input_output_aliases=alias or {},
        compiler_params=pltpu.CompilerParams(vmem_limit_bytes=limit),
        cost_estimate=pl.CostEstimate(flops=flops, bytes_accessed=moved, transcendentals=0),
    )(*ins)


def fetch(owners, q, p, w, qc, pv, sems):
    x, y, c = place()
    one = pltpu.make_async_copy(q.at[at(c * 64, 64), :], qc, sems.at[0])
    two = pltpu.make_async_copy(p, pv, sems.at[1])
    one.start()
    two.start()
    o = owners[c]
    xback = lax.rem(x - o // 8 + 4, 4)
    yback = lax.rem(y - (o // 2) % 4 + 4, 4)
    tests = [o % 2 == c, o % 2 != c] + [xback == d for d in range(4)] + [yback == d for d in range(4)]
    for i, test in enumerate(tests):
        w[i, :, :] = jnp.full((16, 128), jnp.where(test, 1.0, 0.0), F32).astype(BF16)
    one.wait()
    two.wait()


def weigh(w, first, refs, columns):
    total = None
    for d, ref in enumerate(refs):
        term = ref(columns) * w[first + d, 0:1, :]
        total = term if total is None else total + term
    return total


def slices(w, qc, qo, pv, po, a0, a1, a2, a3, b0, b1, b2, b3):
    x, y, c = place()
    for d, a in enumerate((a0, a1, a2, a3)):
        for k in range(4):
            columns = at(lax.rem(x + d, 4) * 512 + 128 * k, 128)
            a[:, 128 * k:128 * k + 128] = weigh(
                w, 0, (lambda s: qc[:, s], lambda s: qo[at(c * 64, 64), s]), columns
            )
    for d, b in enumerate((b0, b1, b2, b3)):
        columns = at(c * 1024 + lax.rem(y + d, 4) * 256, 256)
        b[at(c * 64, 64), :] = pv[:, columns]
        b[at(64 - c * 64, 64), :] = po[:, columns]


def pack(w, a0, a1, a2, a3, b1, b2, b3, g0, g1, r, t1, t2, t3):
    for k in range(4):
        columns = slice(128 * k, 128 * k + 128)
        got = weigh(w, 2, [lambda s, a=a: a[:, s] for a in (a0, a1, a2, a3)], columns)
        for t in (r, t1, t2, t3):
            t[:, columns] = got
    for b, t in ((b1, t1), (b2, t2), (b3, t3)):
        t[:, 512:768] = b[0:64, :]
        t[:, 768:1024] = b[64:128, :]


def pick(w, r, u1, u2, u3, g2, g3, rc):
    for k in range(4):
        columns = slice(128 * k, 128 * k + 128)
        rc[:, columns] = weigh(w, 6, [lambda s, u=u: u[:, s] for u in (r, u1, u2, u3)], columns)


def product(rc, ro, b0, u1, u2, u3, s, raw, block):
    _, y, c = place()
    raw[at(c * 64, 64), :] = rc[...]
    raw[at(64 - c * 64, 64), :] = ro[...]
    block[at(y * 128, 128), :] = b0[...]
    for d, u in enumerate((u1, u2, u3)):
        first = lax.rem(y - (d + 1) + 4, 4) * 128
        block[at(first, 64), :] = u[:, 512:768]
        block[at(first + 64, 64), :] = u[:, 768:1024]
    s[...] = jnp.dot(raw[...], block[...], preferred_element_type=F32)


def round_sum(s0, s1, s2, s3, w):
    w[...] = ((s0[...] + s2[...]) + (s1[...] + s3[...])).astype(BF16)


def join(w, wo, j):
    _, _, c = place()
    layer = lax.axis_index("layer")
    for d in range(4):
        rows = at(lax.rem(layer + d, 4) * 32, 32)
        j[32 * d:32 * d + 32, at(c * 256, 256)] = w[rows, :] * jnp.asarray(0.5, BF16)
        j[32 * d:32 * d + 32, at(256 - c * 256, 256)] = wo[rows, :] * jnp.asarray(0.5, BF16)


SUB = 256


def load(part, store, after, sv, gn, sems):
    copies = []
    for i in range(PART // SUB):
        rows = pl.ds(SUB * i, SUB)
        copies.append(pltpu.make_async_copy(store.at[pl.ds(PART * part + SUB * i, SUB), :], sv.at[rows, :], sems.at[i]))
        copies[-1].start()
    for i in range(PART // SUB):
        copies[i].wait()
        squares = None
        for k in range(16):
            v = sv[SUB * i:SUB * i + SUB, 128 * k:128 * k + 128].astype(F32)
            squares = v * v if squares is None else squares + v * v
        line = jnp.sum(squares.T, axis=0, keepdims=True) * 0.5
        for k in range(SUB // 128):
            row = SUB // 128 * i + k
            gn[row:row + 1, :] = line[:, 128 * k:128 * k + 128]


def term(d, j, sv):
    _, y, _ = place()
    origin = lax.rem(y - d + 4, 4) * 256
    return lax.dot_general(sv[:, at(origin, 256)], j[:, 0:256], NT, preferred_element_type=F32) + lax.dot_general(
        sv[:, at(origin + 1024, 256)], j[:, 256:512], NT, preferred_element_type=F32
    )


def dots_first(j, v0, v1, v2, v3, acc):
    for i, v in enumerate((v0, v1, v2, v3)):
        acc[PART * i:PART * i + PART, :] = term(0, j, v)


def dots_next(d, j, v0, v1, v2, v3, old, acc):
    for i, v in enumerate((v0, v1, v2, v3)):
        rows = slice(PART * i, PART * i + PART)
        acc[rows, :] = old[rows, :] + term(d, j, v)


def dots_last(d, j, j0, ja, jb, v0, v1, v2, v3, old, g0, g1, g2, g3, own, gn, qn, z1, z2, z3):
    zs = (None, z1, z2, z3)
    for i, v in enumerate((v0, v1, v2, v3)):
        rows = slice(PART * i, PART * i + PART)
        out = (old[rows, :] + term(d, j, v)).T
        own[:, rows] = out[0:32, :]
        for e in range(1, 4):
            zs[e][:, rows] = out[32 * e:32 * e + 32, :].astype(BF16)
    total = None
    for piece in (j, j0, ja, jb):
        for k in range(4):
            v = piece[:, 128 * k:128 * k + 128].astype(F32)
            total = v * v if total is None else total + v * v
    qsum = jnp.broadcast_to(jnp.sum(total, axis=1, keepdims=True), (128, 128))
    qn[...] = qsum[0:32, :]
    lane = lax.broadcasted_iota(jnp.int32, (32, 128), 1)
    for e in range(1, 4):
        part = qsum[32 * e:32 * e + 32, :]
        hi = part.astype(BF16).astype(F32)
        zs[e][:, 4352:4480] = jnp.where(lane < 64, hi, part - hi).astype(BF16)
    for i, g in enumerate((g0, g1, g2, g3)):
        gn[8 * i:8 * i + 8, :] = g[...]
    g = gn[...]
    hi = g.astype(BF16)
    lo = (g - hi.astype(F32)).astype(BF16)
    for e in range(1, 4):
        zs[e][:, 4096:4224] = hi
        zs[e][:, 4224:4352] = lo


def finish(own, gn, qn, z1, z2, z3, out):
    g = gn[...]
    q = qn[:, 0:1]
    for z in (z1, z2, z3):
        g = g + (z[:, 4096:4224].astype(F32) + z[:, 4224:4352].astype(F32))
        q = q + (z[:, 4352:4353].astype(F32) + z[:, 4416:4417].astype(F32))
    g = lax.rsqrt(g * 2.0 + 1e-06)
    q = lax.rsqrt(q * 4.0 + 1e-06) * (2.0 * math.sqrt(8192.0))
    for i in range(32):
        columns = slice(128 * i, 128 * i + 128)
        t = (own[:, columns] + z2[:, columns].astype(F32)) + (
            z1[:, columns].astype(F32) + z3[:, columns].astype(F32)
        )
        out[:, columns] = t * g[i:i + 1, :] * q


def moved(dx, dy, dc):
    pairs = []
    for x in range(4):
        for y in range(4):
            for c in range(2):
                to = ((x + dx) % 4 * 4 + (y + dy) % 4) * 2 + (c + dc) % 2
                pairs.append(((x * 4 + y) * 2 + c, to))
    return pairs


def send(a, dx=0, dy=0, dc=0):
    return lax.ppermute(a, "ex", moved(dx, dy, dc))


def send_layer(a, d):
    return lax.ppermute(a, "layer", [(i, (i + d) % 4) for i in range(4)])


def load_part(part, store, after):
    return call(
        lambda *refs: load(part, *refs), "load%d" % part, (store, after),
        [shape((PART, 2048)), shape((8, 128), F32)], spaces={0: HBM, 1: pl.ANY},
        scratch=[pltpu.SemaphoreType.DMA((PART // SUB,))], flops=3 * PART * 2048, moved=8 << 20,
    )


def shards(store, precond, query_slots, owners):
    q = query_slots.reshape(128, 2048)
    p = precond.reshape(64, 2048)
    qo = send(q, dc=1)
    po = send(p, dc=1)
    piece = shape((64, 512))
    block = shape((128, 256))
    w, qc, pv = call(
        fetch, "fetch", (owners, q, p), [shape((10, 16, 128)), shape((64, 2048)), shape((64, 2048))],
        spaces={0: pltpu.SMEM, 1: HBM, 2: HBM}, scratch=[pltpu.SemaphoreType.DMA((2,))],
    )
    a0, a1, a2, a3, b0, b1, b2, b3 = call(slices, "slices", (w, qc, qo, pv, po), [piece] * 4 + [block] * 4)
    v0, g0 = load_part(0, store, a0)
    v1, g1 = load_part(1, store, a0)
    a1, a2, a3 = send(a1, dx=1), send(a2, dx=2), send(a3, dx=3)
    r, t1, t2, t3 = call(
        pack, "pack", (w, a0, a1, a2, a3, b1, b2, b3, g0, g1), [piece] + [shape((64, 1024))] * 3,
        spaces={8: pl.ANY, 9: pl.ANY},
    )
    v2, g2 = load_part(2, store, r)
    v3, g3 = load_part(3, store, r)
    t1, t2, t3 = send(t1, dy=1), send(t2, dy=2), send(t3, dy=3)
    (rc,) = call(pick, "pick", (w, r, t1, t2, t3, g2, g3), [piece], spaces={5: pl.ANY, 6: pl.ANY})
    ro = send(rc, dc=1)
    (s,) = call(
        product, "product", (rc, ro, b0, t1, t2, t3), [shape((128, 256), F32)],
        scratch=[VMEM((128, 512), BF16), VMEM((512, 256), BF16)], flops=2 * 128 * 512 * 256,
    )
    s1, s2, s3 = send(s, dx=1), send(s, dx=2), send(s, dx=3)
    (h,) = call(round_sum, "round_sum", (s, s1, s2, s3), [block])
    ho = send(h, dc=1)
    (j,) = call(join, "join", (h, ho), [shape((128, 512))])
    j1, j2, j3 = send(j, dy=1), send(j, dy=2), send(j, dy=3)
    accs = [shape((4096, 128), F32)]
    work = 2 * 128 * 512 * 4096
    (acc,) = call(dots_first, "dots_first", (j, v0, v1, v2, v3), accs, flops=work)
    for d, piece in ((1, j1), (3, j3)):
        (acc,) = call(
            lambda *refs, d=d: dots_next(d, *refs), "dots_next%d" % d, (piece, v0, v1, v2, v3, acc), accs,
            flops=work, alias={5: 0},
        )
    own, gn, qn, z1, z2, z3 = call(
        lambda *refs: dots_last(2, *refs), "dots_last", (j2, j, j1, j3, v0, v1, v2, v3, acc, g0, g1, g2, g3),
        [shape((32, 4096), F32), shape((32, 128), F32), shape((32, 128), F32)] + [shape((32, 4480))] * 3, flops=work,
    )
    z1, z2, z3 = send_layer(z1, 1), send_layer(z2, 2), send_layer(z3, 3)
    (out,) = call(finish, "finish", (own, gn, qn, z1, z2, z3), [shape((32, 4096), F32)])
    return out.T


def solution(mesh):
    return jax.shard_map(
        shards,
        mesh=mesh,
        in_specs=(P("ex", "layer"), P("layer", "ex", None), P("ex", None, None, "layer"), P()),
        out_specs=P("ex", "layer"),
        check_vma=False,
    )
```

```python
import math

import jax
import jax.numpy as jnp
from jax import lax
from jax.experimental import pallas as pl
from jax.experimental.pallas import tpu as pltpu
from jax.sharding import PartitionSpec as P

BF16, F32 = jnp.bfloat16, jnp.float32
NT = (((1,), (1,)), ((), ()))
VMEM, HBM = pltpu.VMEM, pltpu.HBM
PART = 1024
PARTS = 4


def shape(dims, dtype=BF16):
    return jax.ShapeDtypeStruct(dims, dtype)


def place():
    e = lax.axis_index("ex")
    return e // 8, (e // 2) % 4, e % 2


def at(start, size):
    return pl.ds(pl.multiple_of(start, size), size)


def call(body, name, ins, outs, spaces=None, scratch=(), limit=24 << 20, flops=0, moved=1 << 20, alias=None):
    spaces = spaces or {}
    ins = [
        pltpu.with_memory_space_constraint(a, HBM) if spaces.get(i) in (HBM, pltpu.SMEM) else a
        for i, a in enumerate(ins)
    ]
    return pl.pallas_call(
        body,
        name=name,
        in_specs=[pl.BlockSpec(memory_space=spaces.get(i, VMEM)) for i in range(len(ins))],
        out_specs=[pl.BlockSpec(memory_space=VMEM)] * len(outs),
        out_shape=outs,
        scratch_shapes=scratch,
        input_output_aliases=alias or {},
        compiler_params=pltpu.CompilerParams(vmem_limit_bytes=limit),
        cost_estimate=pl.CostEstimate(flops=flops, bytes_accessed=moved, transcendentals=0),
    )(*ins)


def fetch(owners, q, p, _, w, qc, pv, sems):
    x, y, c = place()
    one = pltpu.make_async_copy(q.at[at(c * 64, 64), :], qc, sems.at[0])
    two = pltpu.make_async_copy(p, pv, sems.at[1])
    one.start()
    two.start()
    o = owners[c]
    xback = lax.rem(x - o // 8 + 4, 4)
    yback = lax.rem(y - (o // 2) % 4 + 4, 4)
    tests = [o % 2 == c, o % 2 != c] + [xback == d for d in range(4)] + [yback == d for d in range(4)]
    for i, test in enumerate(tests):
        w[i, :, :] = jnp.full((16, 128), jnp.where(test, 1.0, 0.0), F32).astype(BF16)
    one.wait()
    two.wait()


def weigh(w, first, refs, columns):
    total = None
    for d, ref in enumerate(refs):
        term = ref(columns) * w[first + d, 0:1, :]
        total = term if total is None else total + term
    return total


def slices(w, qc, qo, pv, po, a0, a1, a2, a3, b0, b1, b2, b3):
    x, y, c = place()
    for d, a in enumerate((a0, a1, a2, a3)):
        for k in range(4):
            columns = at(lax.rem(x + d, 4) * 512 + 128 * k, 128)
            a[:, 128 * k:128 * k + 128] = weigh(
                w, 0, (lambda s: qc[:, s], lambda s: qo[at(c * 64, 64), s]), columns
            )
    for d, b in enumerate((b0, b1, b2, b3)):
        columns = at(c * 1024 + lax.rem(y + d, 4) * 256, 256)
        b[at(c * 64, 64), :] = pv[:, columns]
        b[at(64 - c * 64, 64), :] = po[:, columns]


def pack(w, a0, a1, a2, a3, b1, b2, b3, r, t1, t2, t3):
    for k in range(4):
        columns = slice(128 * k, 128 * k + 128)
        got = weigh(w, 2, [lambda s, a=a: a[:, s] for a in (a0, a1, a2, a3)], columns)
        for t in (r, t1, t2, t3):
            t[:, columns] = got
    for b, t in ((b1, t1), (b2, t2), (b3, t3)):
        t[:, 512:768] = b[0:64, :]
        t[:, 768:1024] = b[64:128, :]


def pick(w, r, u1, u2, u3, g0, rc):
    for k in range(4):
        columns = slice(128 * k, 128 * k + 128)
        rc[:, columns] = weigh(w, 6, [lambda s, u=u: u[:, s] for u in (r, u1, u2, u3)], columns)


def product(rc, ro, b0, u1, u2, u3, s, raw, block):
    _, y, c = place()
    raw[at(c * 64, 64), :] = rc[...]
    raw[at(64 - c * 64, 64), :] = ro[...]
    block[at(y * 128, 128), :] = b0[...]
    for d, u in enumerate((u1, u2, u3)):
        first = lax.rem(y - (d + 1) + 4, 4) * 128
        block[at(first, 64), :] = u[:, 512:768]
        block[at(first + 64, 64), :] = u[:, 768:1024]
    s[...] = jnp.dot(raw[...], block[...], preferred_element_type=F32)


def round_sum(s0, s1, s2, s3, g1, h):
    layer = lax.axis_index("layer")
    for d in range(4):
        rows = at(lax.rem(layer + d, 4) * 32, 32)
        total = ((s0[rows, :] + s2[rows, :]) + (s1[rows, :] + s3[rows, :])).astype(BF16)
        h[32 * d:32 * d + 32, :] = total * jnp.asarray(0.5, BF16)


def join(h, o, _, j):
    _, _, c = place()
    j[:, at(c * 256, 256)] = h[...]
    j[:, at(256 - c * 256, 256)] = o[...]


def norms(part, v, after, gn):
    for i in range(8):
        rows = slice(2048 * part + 256 * i, 2048 * part + 256 * i + 256)
        squares = None
        for k in range(16):
            t = v[rows, 128 * k:128 * k + 128].astype(F32)
            squares = t * t if squares is None else squares + t * t
        line = jnp.sum(squares.T, axis=0, keepdims=True) * 0.5
        for k in range(2):
            gn[2 * i + k:2 * i + k + 1, :] = line[:, 128 * k:128 * k + 128]


def term(d, half, h, v, rows):
    _, y, _ = place()
    columns = at(half * 1024 + lax.rem(y - d + 4, 4) * 256, 256)
    return lax.dot_general(v[rows, columns], h, NT, preferred_element_type=F32)


def both(d, j, v, rows):
    return term(d, 0, j[:, 0:256], v, rows) + term(d, 1, j[:, 256:512], v, rows)


def dots_own(h, v, acc):
    _, _, c = place()
    for i in range(PARTS):
        rows = slice(PART * i, PART * i + PART)
        acc[rows, :] = term(0, c, h[...], v, rows)


def dots_other(h, v, old, acc):
    _, _, c = place()
    for i in range(PARTS):
        rows = slice(PART * i, PART * i + PART)
        acc[rows, :] = old[rows, :] + term(0, 1 - c, h[...], v, rows)


def dots_next(d, j, v, old, acc):
    for i in range(PARTS):
        rows = slice(PART * i, PART * i + PART)
        acc[rows, :] = old[rows, :] + both(d, j, v, rows)


def dots_half(d, first, j, v, old, own, z1, z2, z3):
    for i in range(2):
        rows = slice(first + PART * i, first + PART * i + PART)
        columns = slice(PART * i, PART * i + PART)
        out = (old[rows, :] + both(d, j, v, rows)).T
        own[:, columns] = out[0:32, :]
        for e, z in ((1, z1), (2, z2), (3, z3)):
            z[:, columns] = out[32 * e:32 * e + 32, :].astype(BF16)


def extras(pieces, gs, gn, qn, z1, z2, z3):
    total = None
    for piece in pieces:
        for k in range(4):
            v = piece[:, 128 * k:128 * k + 128].astype(F32)
            total = v * v if total is None else total + v * v
    qsum = jnp.broadcast_to(jnp.sum(total, axis=1, keepdims=True), (128, 128))
    qn[...] = qsum[0:32, :]
    for i, g in enumerate(gs):
        gn[16 * i:16 * i + 16, :] = g[...]
    g = gn[...]
    hi = g.astype(BF16)
    lo = (g - hi.astype(F32)).astype(BF16)
    lane = lax.broadcasted_iota(jnp.int32, (32, 128), 1)
    for e, z in ((1, z1), (2, z2), (3, z3)):
        part = qsum[32 * e:32 * e + 32, :]
        top = part.astype(BF16).astype(F32)
        z[:, 2048:2176] = hi
        z[:, 2176:2304] = lo
        z[:, 2304:2432] = jnp.where(lane < 64, top, part - top).astype(BF16)


def scales(gn, qn, z1, z2, z3, g_ref, q_ref):
    g = gn[...]
    q = qn[:, 0:1]
    for z in (z1, z2, z3):
        g = g + (z[:, 2048:2176].astype(F32) + z[:, 2176:2304].astype(F32))
        q = q + (z[:, 2304:2305].astype(F32) + z[:, 2368:2369].astype(F32))
    g_ref[...] = lax.rsqrt(g * 2.0 + 1e-06)
    q = lax.rsqrt(q * 4.0 + 1e-06) * (2.0 * math.sqrt(8192.0))
    q_ref[...] = jnp.broadcast_to(q, (32, 128))


def finish(first, own, g, q, z1, z2, z3, out, part, sem):
    scale = q[...]
    for i in range(16):
        columns = slice(128 * i, 128 * i + 128)
        t = (own[:, columns] + z2[:, columns].astype(F32)) + (
            z1[:, columns].astype(F32) + z3[:, columns].astype(F32)
        )
        row = first // 128 + i
        part[:, columns] = t * g[row:row + 1, :] * scale
    copy = pltpu.make_async_copy(part, out.at[:, pl.ds(first, 2048)], sem)
    copy.start()
    copy.wait()


def finish_first(own, gn, qn, z1, z2, z3, out, g, q, part, sem):
    scales(gn, qn, z1, z2, z3, g, q)
    finish(0, own, g, q, z1, z2, z3, out, part, sem)


def finish_second(own, g, q, z1, z2, z3, _, out, part, sem):
    finish(2048, own, g, q, z1, z2, z3, out, part, sem)


def moved(dx, dy, dc):
    pairs = []
    for x in range(4):
        for y in range(4):
            for c in range(2):
                to = ((x + dx) % 4 * 4 + (y + dy) % 4) * 2 + (c + dc) % 2
                pairs.append(((x * 4 + y) * 2 + c, to))
    return pairs


def send(a, dx=0, dy=0, dc=0):
    return lax.ppermute(a, "ex", moved(dx, dy, dc))


def send_layer(a, d):
    return lax.ppermute(a, "layer", [(i, (i + d) % 4) for i in range(4)])


def norms_part(part, store, after):
    return call(
        lambda *refs: norms(part, *refs), "norms%d" % part, (store, after), [shape((16, 128), F32)],
        spaces={1: pl.ANY}, flops=3 * 2048 * 2048, moved=8 << 20,
    )[0]


def shards(store, precond, query_slots, owners):

    q = query_slots.reshape(128, 2048)
    p = precond.reshape(64, 2048)
    qo = send(q, dc=1)
    po = send(p, dc=1)
    piece = shape((64, 512))
    block = shape((128, 256))
    w, qc, pv = call(
        fetch, "fetch", (owners, q, p, store), [shape((10, 16, 128)), shape((64, 2048)), shape((64, 2048))],
        spaces={0: pltpu.SMEM, 1: HBM, 2: HBM, 3: HBM}, scratch=[pltpu.SemaphoreType.DMA((2,))],
    )
    a0, a1, a2, a3, b0, b1, b2, b3 = call(slices, "slices", (w, qc, qo, pv, po), [piece] * 4 + [block] * 4)
    a1, a2, a3 = send(a1, dx=1), send(a2, dx=2), send(a3, dx=3)
    r, t1, t2, t3 = call(
        pack, "pack", (w, a0, a1, a2, a3, b1, b2, b3), [piece] + [shape((64, 1024))] * 3,
    )
    g0 = norms_part(0, store, r)
    t1, t2, t3 = send(t1, dy=1), send(t2, dy=2), send(t3, dy=3)
    (rc,) = call(pick, "pick", (w, r, t1, t2, t3, g0), [piece], spaces={5: pl.ANY})
    ro = send(rc, dc=1)
    (s,) = call(
        product, "product", (rc, ro, b0, t1, t2, t3), [shape((128, 256), F32)],
        scratch=[VMEM((128, 512), BF16), VMEM((512, 256), BF16)], flops=2 * 128 * 512 * 256,
    )
    g1 = norms_part(1, store, s)
    s1, s2, s3 = send(s, dx=1), send(s, dx=2), send(s, dx=3)
    (h,) = call(round_sum, "round_sum", (s, s1, s2, s3, g1), [block], spaces={4: pl.ANY})
    o = send(h, dc=1)
    accs = [shape((4096, 128), F32)]
    (acc,) = call(dots_own, "dots_own", (h, store), accs, flops=2 * 128 * 256 * 4096)
    (j,) = call(join, "join", (h, o, acc), [shape((128, 512))], spaces={2: pl.ANY})
    j1, j2, j3 = send(j, dy=1), send(j, dy=2), send(j, dy=3)
    (acc,) = call(dots_other, "dots_other", (o, store, acc), accs, flops=2 * 128 * 256 * 4096, alias={2: 0})
    for d, piece in ((1, j1), (3, j3)):
        (acc,) = call(
            lambda *f, d=d: dots_next(d, *f), "dots_next%d" % d, (piece, store, acc), accs,
            flops=2 * 128 * 512 * 4096, alias={2: 0},
        )
    half = shape((32, 2048), F32)

    def first_half(k, j0, ja, jb, v, old, g0, g1, own, gn, qn, z1, z2, z3):
        dots_half(2, 0, k, v, old, own, z1, z2, z3)
        extras((k, j0, ja, jb), (g0, g1), gn, qn, z1, z2, z3)

    own_a, gn, qn, a1, a2, a3 = call(
        first_half, "dots_first_half", (j2, j, j1, j3, store, acc, g0, g1),
        [half, shape((32, 128), F32), shape((32, 128), F32)] + [shape((32, 2432))] * 3, flops=128 * 512 * 4096,
    )

    def second_half(k, v, old, _, own, z1, z2, z3):
        dots_half(2, 2048, k, v, old, own, z1, z2, z3)

    own_b, b1, b2, b3 = call(
        second_half, "dots_second_half", (j2, store, acc, gn), [half] + [shape((32, 2048))] * 3,
        spaces={3: pl.ANY}, flops=128 * 512 * 4096,
    )
    a1, a3, a2 = send_layer(a1, 1), send_layer(a3, 3), send_layer(a2, 2)
    b1, b3, b2 = send_layer(b1, 1), send_layer(b3, 3), send_layer(b2, 2)
    params = pltpu.CompilerParams(vmem_limit_bytes=24 << 20)
    vm, hbm = pl.BlockSpec(memory_space=VMEM), pl.BlockSpec(memory_space=pl.ANY)
    scratch = [VMEM((32, 2048), F32), pltpu.SemaphoreType.DMA(())]
    full = shape((32, 4096), F32)
    out, g, q = pl.pallas_call(
        finish_first, name="finish_first", in_specs=[vm] * 6, out_specs=[hbm, vm, vm],
        out_shape=[full, shape((32, 128), F32), shape((32, 128), F32)], scratch_shapes=scratch, compiler_params=params,
    )(own_a, gn, qn, a1, a2, a3)
    out = pl.pallas_call(
        finish_second, name="finish_second", in_specs=[vm] * 6 + [hbm], out_specs=hbm, out_shape=full,
        scratch_shapes=scratch, compiler_params=params, input_output_aliases={6: 0},
    )(own_b, g, q, b1, b2, b3, out)
    return out.T


def solution(mesh):
    return jax.shard_map(
        shards,
        mesh=mesh,
        in_specs=(P("ex", "layer"), P("layer", "ex", None), P("ex", None, None, "layer"), P()),
        out_specs=P("ex", "layer"),
        check_vma=False,
    )
```

```python
import math

import jax
import jax.numpy as jnp
from jax import lax
from jax.experimental import pallas as pl
from jax.experimental.pallas import tpu as pltpu
from jax.sharding import PartitionSpec as P

BF16, F32 = jnp.bfloat16, jnp.float32
NT = (((1,), (1,)), ((), ()))
VMEM, HBM = pltpu.VMEM, pltpu.HBM
PART = 1024
PARTS = 4


def shape(dims, dtype=BF16):
    return jax.ShapeDtypeStruct(dims, dtype)


def place():
    e = lax.axis_index("ex")
    return e // 8, (e // 2) % 4, e % 2


def at(start, size):
    return pl.ds(pl.multiple_of(start, size), size)


def call(body, name, ins, outs, spaces=None, scratch=(), limit=24 << 20, flops=0, moved=1 << 20, alias=None):
    spaces = spaces or {}
    ins = [
        pltpu.with_memory_space_constraint(a, HBM) if spaces.get(i) in (HBM, pltpu.SMEM) else a
        for i, a in enumerate(ins)
    ]
    return pl.pallas_call(
        body,
        name=name,
        in_specs=[pl.BlockSpec(memory_space=spaces.get(i, VMEM)) for i in range(len(ins))],
        out_specs=[pl.BlockSpec(memory_space=VMEM)] * len(outs),
        out_shape=outs,
        scratch_shapes=scratch,
        input_output_aliases=alias or {},
        compiler_params=pltpu.CompilerParams(vmem_limit_bytes=limit),
        cost_estimate=pl.CostEstimate(flops=flops, bytes_accessed=moved, transcendentals=0),
    )(*ins)


def fetch(owners, q, p, _, w, qc, pv, sems):
    x, y, c = place()
    one = pltpu.make_async_copy(q.at[at(c * 64, 64), :], qc, sems.at[0])
    two = pltpu.make_async_copy(p, pv, sems.at[1])
    one.start()
    two.start()
    o = owners[c]
    xback = lax.rem(x - o // 8 + 4, 4)
    yback = lax.rem(y - (o // 2) % 4 + 4, 4)
    tests = [o % 2 == c, o % 2 != c] + [xback == d for d in range(4)] + [yback == d for d in range(4)]
    for i, test in enumerate(tests):
        w[i, :, :] = jnp.full((16, 128), jnp.where(test, 1.0, 0.0), F32).astype(BF16)
    one.wait()
    two.wait()


def weigh(w, first, refs, columns):
    total = None
    for d, ref in enumerate(refs):
        term = ref(columns) * w[first + d, 0:1, :]
        total = term if total is None else total + term
    return total


def slices(w, qc, qo, pv, po, a0, a1, a2, a3, b0, b1, b2, b3):
    x, y, c = place()
    for d, a in enumerate((a0, a1, a2, a3)):
        for k in range(4):
            columns = at(lax.rem(x + d, 4) * 512 + 128 * k, 128)
            a[:, 128 * k:128 * k + 128] = weigh(
                w, 0, (lambda s: qc[:, s], lambda s: qo[at(c * 64, 64), s]), columns
            )
    for d, b in enumerate((b0, b1, b2, b3)):
        columns = at(lax.rem(y + d, 4) * 512, 512)
        b[at(c * 64, 64), :] = pv[:, columns]
        b[at(64 - c * 64, 64), :] = po[:, columns]


def pack(w, a0, a1, a2, a3, b1, b2, b3, r, t1, t2, t3):
    for k in range(4):
        columns = slice(128 * k, 128 * k + 128)
        got = weigh(w, 2, [lambda s, a=a: a[:, s] for a in (a0, a1, a2, a3)], columns)
        for t in (r, t1, t2, t3):
            t[:, columns] = got
    for b, t in ((b1, t1), (b2, t2), (b3, t3)):
        t[:, 512:1024] = b[0:64, :]
        t[:, 1024:1536] = b[64:128, :]


def product(w, r, b0, u1, u2, u3, _, s, s1, s2, s3, raw, block):
    _, y, _ = place()
    for k in range(4):
        columns = slice(128 * k, 128 * k + 128)
        raw[:, columns] = weigh(w, 6, [lambda s, u=u: u[:, s] for u in (r, u1, u2, u3)], columns)
    block[at(y * 128, 128), :] = b0[...]
    for d, u in enumerate((u1, u2, u3)):
        first = lax.rem(y - (d + 1) + 4, 4) * 128
        block[at(first, 64), :] = u[:, 512:1024]
        block[at(first + 64, 64), :] = u[:, 1024:1536]
    total = jnp.dot(raw[...], block[...], preferred_element_type=F32)
    for ref in (s, s1, s2, s3):
        ref[...] = total


def round_sum(s0, s1, s2, s3, _, h):
    total = ((s0[...] + s2[...]) + (s1[...] + s3[...])).astype(BF16)
    h[...] = total * jnp.asarray(0.5, BF16)


def join(h, o, j1, j3, j2):
    _, _, c = place()
    layer = lax.axis_index("layer")
    for ref, block in ((h, c), (o, 1 - c)):
        for t in range(2):
            rows = at(lax.rem(2 * block + t - layer + 4, 4) * 32, 32)
            for j in (j1, j3, j2):
                j[rows, :] = ref[32 * t:32 * t + 32, :]


def norms(part, v, after, gn):
    for i in range(8):
        rows = slice(2048 * part + 256 * i, 2048 * part + 256 * i + 256)
        squares = None
        for k in range(16):
            t = v[rows, 128 * k:128 * k + 128].astype(F32)
            squares = t * t if squares is None else squares + t * t
        line = jnp.sum(squares.T, axis=0, keepdims=True) * 0.5
        for k in range(2):
            gn[2 * i + k:2 * i + k + 1, :] = line[:, 128 * k:128 * k + 128]


def term(d, j, v, rows):
    _, y, _ = place()
    columns = at(lax.rem(y - d + 4, 4) * 512, 512)
    return lax.dot_general(v[rows, columns], j[...], NT, preferred_element_type=F32)


def dots_first(j, v, acc):
    for i in range(PARTS):
        rows = slice(PART * i, PART * i + PART)
        acc[rows, :] = term(0, j, v, rows)


def dots_next(d, j, v, old, acc):
    for i in range(PARTS):
        rows = slice(PART * i, PART * i + PART)
        acc[rows, :] = old[rows, :] + term(d, j, v, rows)


def dots_last(d, j, j0, ja, jb, v, old, g0, g1, own, gn, qn, z1, z3, z2):
    zs = ((1, z1), (2, z2), (3, z3))
    for i in range(PARTS):
        rows = slice(PART * i, PART * i + PART)
        out = (old[rows, :] + term(d, j, v, rows)).T
        own[:, rows] = out[0:32, :]
        for e, z in zs:
            z[:, rows] = out[32 * e:32 * e + 32, :].astype(BF16)
    total = None
    for piece in (j, j0, ja, jb):
        for k in range(4):
            t = piece[:, 128 * k:128 * k + 128].astype(F32)
            total = t * t if total is None else total + t * t
    qsum = jnp.broadcast_to(jnp.sum(total, axis=1, keepdims=True), (128, 128))
    qn[...] = qsum[0:32, :]
    for i, g in enumerate((g0, g1)):
        gn[16 * i:16 * i + 16, :] = g[...]
    g = gn[...]
    hi = g.astype(BF16)
    lo = (g - hi.astype(F32)).astype(BF16)
    lane = lax.broadcasted_iota(jnp.int32, (32, 128), 1)
    for e, z in zs:
        part = qsum[32 * e:32 * e + 32, :]
        top = part.astype(BF16).astype(F32)
        z[:, 4096:4224] = hi
        z[:, 4224:4352] = lo
        z[:, 4352:4480] = jnp.where(lane < 64, top, part - top).astype(BF16)


def norm_parts(z):
    return (
        z[:, 4096:4224].astype(F32) + z[:, 4224:4352].astype(F32),
        z[:, 4352:4353].astype(F32) + z[:, 4416:4417].astype(F32),
    )


def finish_first(own, gn, qn, z1, z3, t, g, q):
    g1, q1 = norm_parts(z1)
    g3, q3 = norm_parts(z3)
    g[...] = gn[...] + (g1 + g3)
    q[...] = jnp.broadcast_to(qn[:, 0:1] + (q1 + q3), (32, 128))
    for i in range(32):
        columns = slice(128 * i, 128 * i + 128)
        t[:, columns] = own[:, columns] + (z1[:, columns].astype(F32) + z3[:, columns].astype(F32))


def finish_last(t, g, q, z2, out, part, sems):
    g2, q2 = norm_parts(z2)
    g = lax.rsqrt((g[...] + g2) * 2.0 + 1e-06)
    q = lax.rsqrt((q[:, 0:1] + q2) * 4.0 + 1e-06) * (2.0 * math.sqrt(8192.0))
    copies = []
    for n in range(4):
        for i in range(8 * n, 8 * n + 8):
            columns = slice(128 * i, 128 * i + 128)
            part[:, columns] = (t[:, columns] + z2[:, columns].astype(F32)) * g[i:i + 1, :] * q
        columns = pl.ds(1024 * n, 1024)
        copies.append(pltpu.make_async_copy(part.at[:, columns], out.at[:, columns], sems.at[n]))
        copies[-1].start()
    for copy in copies:
        copy.wait()


def moved(dx, dy, dc):
    pairs = []
    for x in range(4):
        for y in range(4):
            for c in range(2):
                to = ((x + dx) % 4 * 4 + (y + dy) % 4) * 2 + (c + dc) % 2
                pairs.append(((x * 4 + y) * 2 + c, to))
    return pairs


def send(a, dx=0, dy=0, dc=0):
    return lax.ppermute(a, "ex", moved(dx, dy, dc))


def send_layer(a, d):
    return lax.ppermute(a, "layer", [(i, (i + d) % 4) for i in range(4)])


def norms_part(part, store, after):
    return call(
        lambda *refs: norms(part, *refs), "norms%d" % part, (store, after), [shape((16, 128), F32)],
        spaces={1: pl.ANY}, flops=3 * 2048 * 2048, moved=8 << 20,
    )[0]


def shards(store, precond, query_slots, owners):

    q = query_slots.reshape(128, 2048)
    p = precond.reshape(64, 2048)
    qo = send(q, dc=1)
    po = send(p, dc=1)
    piece = shape((64, 512))
    block = shape((128, 512))
    w, qc, pv = call(
        fetch, "fetch", (owners, q, p, store), [shape((10, 16, 128)), shape((64, 2048)), shape((64, 2048))],
        spaces={0: pltpu.SMEM, 1: HBM, 2: HBM, 3: HBM}, scratch=[pltpu.SemaphoreType.DMA((2,))],
    )
    a0, a1, a2, a3, b0, b1, b2, b3 = call(slices, "slices", (w, qc, qo, pv, po), [piece] * 4 + [block] * 4)
    a1, a2, a3 = send(a1, dx=1), send(a2, dx=2), send(a3, dx=3)
    r, t1, t2, t3 = call(
        pack, "pack", (w, a0, a1, a2, a3, b1, b2, b3), [piece] + [shape((64, 1536))] * 3,
    )
    g0 = norms_part(0, store, r)
    t1, t2, t3 = send(t1, dy=1), send(t2, dy=2), send(t3, dy=3)
    s, s1, s2, s3 = call(
        product, "product", (w, r, b0, t1, t2, t3, g0), [shape((64, 512), F32)] * 4, spaces={6: pl.ANY},
        scratch=[VMEM((64, 512), BF16), VMEM((512, 512), BF16)], flops=2 * 64 * 512 * 512,
    )
    g1 = norms_part(1, store, s)
    s1, s2, s3 = send(s1, dx=1), send(s2, dx=2), send(s3, dx=3)
    (h,) = call(round_sum, "round_sum", (s, s1, s2, s3, g1), [piece], spaces={4: pl.ANY})
    o = send(h, dc=1)
    j1, j3, j2 = call(join, "join", (h, o), [shape((128, 512))] * 3)
    j = j1
    j1, j3, j2 = send(j1, dy=1), send(j3, dy=3), send(j2, dy=2)
    accs = [shape((4096, 128), F32)]
    work = 2 * 128 * 512 * 4096
    (acc,) = call(dots_first, "dots_first", (j, store), accs, flops=work)
    for d, got in ((1, j1), (3, j3)):
        (acc,) = call(
            lambda *f, d=d: dots_next(d, *f), "dots_next%d" % d, (got, store, acc), accs, flops=work, alias={2: 0},
        )
    norm = shape((32, 128), F32)
    own, gn, qn, z1, z3, z2 = call(
        lambda *f: dots_last(2, *f), "dots_last", (j2, j, j1, j3, store, acc, g0, g1),
        [shape((32, 4096), F32), norm, norm] + [shape((32, 4480))] * 3, flops=work,
    )
    z1, z3, z2 = send_layer(z1, 1), send_layer(z3, 3), send_layer(z2, 2)
    t, g, q = call(finish_first, "finish_first", (own, gn, qn, z1, z3), [shape((32, 4096), F32), norm, norm])
    out = pl.pallas_call(
        finish_last,
        name="finish_last",
        in_specs=[pl.BlockSpec(memory_space=VMEM)] * 4,
        out_specs=pl.BlockSpec(memory_space=pl.ANY),
        out_shape=shape((32, 4096), F32),
        scratch_shapes=[VMEM((32, 4096), F32), pltpu.SemaphoreType.DMA((4,))],
        compiler_params=pltpu.CompilerParams(vmem_limit_bytes=24 << 20),
    )(t, g, q, z2)
    return out.T


def solution(mesh):
    return jax.shard_map(
        shards,
        mesh=mesh,
        in_specs=(P("ex", "layer"), P("layer", "ex", None), P("ex", None, None, "layer"), P()),
        out_specs=P("ex", "layer"),
        check_vma=False,
    )
```

```python
import math

import jax
import jax.numpy as jnp
from jax import lax
from jax.experimental import pallas as pl
from jax.experimental.pallas import tpu as pltpu
from jax.sharding import PartitionSpec as P

BF16, F32 = jnp.bfloat16, jnp.float32
NT = (((1,), (1,)), ((), ()))
VMEM, HBM = pltpu.VMEM, pltpu.HBM
PART = 1024
PARTS = 4


def shape(dims, dtype=BF16):
    return jax.ShapeDtypeStruct(dims, dtype)


def place():
    e = lax.axis_index("ex")
    return e // 8, (e // 2) % 4, e % 2


def at(start, size):
    return pl.ds(pl.multiple_of(start, size), size)


def call(body, name, ins, outs, spaces=None, scratch=(), limit=24 << 20, flops=0, moved=1 << 20, alias=None):
    spaces = spaces or {}
    ins = [
        pltpu.with_memory_space_constraint(a, HBM) if spaces.get(i) is HBM else a
        for i, a in enumerate(ins)
    ]
    return pl.pallas_call(
        body,
        name=name,
        in_specs=[pl.BlockSpec(memory_space=spaces.get(i, VMEM)) for i in range(len(ins))],
        out_specs=[pl.BlockSpec(memory_space=VMEM)] * len(outs),
        out_shape=outs,
        scratch_shapes=scratch,
        input_output_aliases=alias or {},
        compiler_params=pltpu.CompilerParams(vmem_limit_bytes=limit),
        cost_estimate=pl.CostEstimate(flops=flops, bytes_accessed=moved, transcendentals=0),
    )(*ins)


def fetch(owners, q, p, w, qc, pv, o_ref, sems):
    x, y, c = place()
    copies = [
        pltpu.make_async_copy(owners, o_ref, sems.at[0]),
        pltpu.make_async_copy(q.at[at(c * 64, 64), :], qc, sems.at[1]),
        pltpu.make_async_copy(p, pv, sems.at[2]),
    ]
    for copy in copies:
        copy.start()
    copies[0].wait()
    o = o_ref[c]
    xback = lax.rem(x - o // 8 + 4, 4)
    yback = lax.rem(y - (o // 2) % 4 + 4, 4)
    tests = [o % 2 == c, o % 2 != c] + [xback == d for d in range(4)] + [yback == d for d in range(4)]
    for i, test in enumerate(tests):
        w[i, :, :] = jnp.full((16, 128), jnp.where(test, 1.0, 0.0), F32).astype(BF16)
    copies[1].wait()
    copies[2].wait()


def weigh(w, first, refs, columns):
    total = None
    for d, ref in enumerate(refs):
        term = ref(columns) * w[first + d, 0:1, :]
        total = term if total is None else total + term
    return total


def slices(w, qc, qo, _, a0, a1, a2, a3):
    x, _, c = place()
    for d, a in enumerate((a0, a1, a2, a3)):
        for k in range(4):
            columns = at(lax.rem(x + d, 4) * 512 + 128 * k, 128)
            a[:, 128 * k:128 * k + 128] = weigh(
                w, 0, (lambda s: qc[:, s], lambda s: qo[at(c * 64, 64), s]), columns
            )


def cut(pv, _, b0, b1, b2, b3):
    _, y, _ = place()
    for d, b in enumerate((b0, b1, b2, b3)):
        b[...] = pv[:, at(lax.rem(y + d, 4) * 512, 512)]


def choose(w, a0, a1, a2, a3, r1, r2, r3):
    for k in range(4):
        columns = slice(128 * k, 128 * k + 128)
        got = weigh(w, 2, [lambda s, a=a: a[:, s] for a in (a0, a1, a2, a3)], columns)
        for r in (r1, r2, r3):
            r[:, columns] = got


def pick(w, r, u1, u2, u3, raw):
    for k in range(4):
        columns = slice(128 * k, 128 * k + 128)
        raw[:, columns] = weigh(w, 6, [lambda s, u=u: u[:, s] for u in (r, u1, u2, u3)], columns)


def product(raw, po, b0, b1, b2, b3, o1, o2, o3, s, s1, s2, s3, block):
    _, y, c = place()
    for d, (b, o) in enumerate(((b0, None), (b1, o1), (b2, o2), (b3, o3))):
        first = lax.rem(y - d + 4, 4) * 128
        block[at(first + c * 64, 64), :] = b[...]
        block[at(first + 64 - c * 64, 64), :] = po[:, at(y * 512, 512)] if o is None else o[...]
    total = jnp.dot(raw[...], block[...], preferred_element_type=F32)
    for ref in (s, s1, s2, s3):
        ref[...] = total


def round_sum(s0, s1, s2, s3, _, __, h):
    total = ((s0[...] + s2[...]) + (s1[...] + s3[...])).astype(BF16)
    h[...] = total * jnp.asarray(0.5, BF16)


WAYS = ((1, 3, 2), (2, 1, 3))


def slot(ahead, c):
    found = 0
    for k in range(3):
        found = jnp.where(ahead == jnp.where(c == 0, WAYS[0][k], WAYS[1][k]), k + 1, found)
    return found


def join(h, o, j1, j3, j2):
    _, _, c = place()
    layer = lax.axis_index("layer")
    for ref, block in ((h, c), (o, 1 - c)):
        for t in range(2):
            rows = at(slot(lax.rem(2 * block + t - layer + 4, 4), c) * 32, 32)
            for j in (j1, j3, j2):
                j[rows, :] = ref[32 * t:32 * t + 32, :]


def norms(part, v, after, gn):
    for i in range(8):
        rows = slice(2048 * part + 256 * i, 2048 * part + 256 * i + 256)
        squares = None
        for k in range(16):
            t = v[rows, 128 * k:128 * k + 128].astype(F32)
            squares = t * t if squares is None else squares + t * t
        line = jnp.sum(squares.T, axis=0, keepdims=True) * 0.5
        for k in range(2):
            gn[2 * i + k:2 * i + k + 1, :] = line[:, 128 * k:128 * k + 128]


def term(d, j, v, rows):
    _, y, _ = place()
    columns = at(lax.rem(y - d + 4, 4) * 512, 512)
    return lax.dot_general(v[rows, columns], j[...], NT, preferred_element_type=F32)


def dots_first(j, v, acc):
    for i in range(PARTS):
        rows = slice(PART * i, PART * i + PART)
        acc[rows, :] = term(0, j, v, rows)


def dots_next(d, j, v, old, acc):
    for i in range(PARTS):
        rows = slice(PART * i, PART * i + PART)
        acc[rows, :] = old[rows, :] + term(d, j, v, rows)


def dots_last(d, j, j0, ja, jb, v, old, g0, g1, own, gn, qn, z1, z2, z3):
    zs = ((1, z1), (2, z2), (3, z3))
    for i in range(PARTS):
        rows = slice(PART * i, PART * i + PART)
        out = (old[rows, :] + term(d, j, v, rows)).T
        own[:, rows] = out[0:32, :]
        for e, z in zs:
            z[:, rows] = out[32 * e:32 * e + 32, :].astype(BF16)
    total = None
    for piece in (j, j0, ja, jb):
        for k in range(4):
            t = piece[:, 128 * k:128 * k + 128].astype(F32)
            total = t * t if total is None else total + t * t
    qsum = jnp.broadcast_to(jnp.sum(total, axis=1, keepdims=True), (128, 128))
    qn[...] = qsum[0:32, :]
    for i, g in enumerate((g0, g1)):
        gn[16 * i:16 * i + 16, :] = g[...]
    lane = lax.broadcasted_iota(jnp.int32, (32, 128), 1)
    for e, z in zs:
        part = qsum[32 * e:32 * e + 32, :]
        top = part.astype(BF16).astype(F32)
        z[:, 4096:4224] = gn[...].astype(BF16)
        z[:, 4224:4352] = jnp.where(lane < 64, top, part - top).astype(BF16)


def norm_parts(z):
    return z[:, 4096:4224].astype(F32), z[:, 4224:4225].astype(F32) + z[:, 4288:4289].astype(F32)


def finish_first(own, gn, qn, z1, z3, t, g, q):
    g1, q1 = norm_parts(z1)
    g3, q3 = norm_parts(z3)
    g[...] = gn[...] + (g1 + g3)
    q[...] = jnp.broadcast_to(qn[:, 0:1] + (q1 + q3), (32, 128))
    for i in range(32):
        columns = slice(128 * i, 128 * i + 128)
        t[:, columns] = own[:, columns] + (z1[:, columns].astype(F32) + z3[:, columns].astype(F32))


def finish_last(t, g, q, z2, out, part, sems):
    g2, q2 = norm_parts(z2)
    g = lax.rsqrt((g[...] + g2) * 2.0 + 1e-06)
    q = lax.rsqrt((q[:, 0:1] + q2) * 4.0 + 1e-06) * (2.0 * math.sqrt(8192.0))
    copies = []
    for n in range(4):
        for i in range(8 * n, 8 * n + 8):
            columns = slice(128 * i, 128 * i + 128)
            part[:, columns] = (t[:, columns] + z2[:, columns].astype(F32)) * g[i:i + 1, :] * q
        columns = pl.ds(1024 * n, 1024)
        copies.append(pltpu.make_async_copy(part.at[:, columns], out.at[:, columns], sems.at[n]))
        copies[-1].start()
    for copy in copies:
        copy.wait()


def moved(dx, dy, dc):
    pairs = []
    for x in range(4):
        for y in range(4):
            for c in range(2):
                to = ((x + dx) % 4 * 4 + (y + dy) % 4) * 2 + (c + dc) % 2
                pairs.append(((x * 4 + y) * 2 + c, to))
    return pairs


def send(a, dx=0, dy=0, dc=0):
    return lax.ppermute(a, "ex", moved(dx, dy, dc))


def send_layer(a, k):
    pairs = []
    for e in range(32):
        for layer in range(4):
            pairs.append((4 * e + layer, 4 * e + (layer + WAYS[e % 2][k]) % 4))
    return lax.ppermute(a, ("ex", "layer"), pairs)


def norms_part(part, store, after):
    return call(
        lambda *refs: norms(part, *refs), "norms%d" % part, (store, after), [shape((16, 128), F32)],
        spaces={1: pl.ANY}, flops=3 * 2048 * 2048, moved=8 << 20,
    )[0]


def shards(store, precond, query_slots, owners):
    q = query_slots.reshape(128, 2048)
    p = precond.reshape(64, 2048)
    qo = send(q, dc=1)
    po = send(p, dc=1)
    piece = shape((64, 512))
    w, qc, pv = call(
        fetch, "fetch", (owners, q, p), [shape((10, 16, 128)), shape((64, 2048)), shape((64, 2048))],
        spaces={0: HBM, 1: HBM, 2: HBM}, scratch=[pltpu.SMEM((2,), jnp.int32), pltpu.SemaphoreType.DMA((3,))],
    )
    a0, a1, a2, a3 = call(slices, "slices", (w, qc, qo, store), [piece] * 4, spaces={3: HBM})
    a1, a2, a3 = send(a1, dx=1), send(a2, dx=2), send(a3, dx=3)
    b0, b1, b2, b3 = call(cut, "cut", (pv, a0), [piece] * 4, spaces={1: pl.ANY})
    b1, b2, b3 = send(b1, dy=1), send(b2, dy=2), send(b3, dy=3)
    r1, r2, r3 = call(choose, "choose", (w, a0, a1, a2, a3), [piece] * 3)
    r = r1
    r1, r2, r3 = send(r1, dy=1), send(r2, dy=2), send(r3, dy=3)
    o1, o2, o3 = send(b1, dc=1), send(b2, dc=1), send(b3, dc=1)
    (raw,) = call(pick, "pick", (w, r, r1, r2, r3), [piece])
    s, s1, s2, s3 = call(
        product, "product", (raw, po, b0, b1, b2, b3, o1, o2, o3), [shape((64, 512), F32)] * 4,
        scratch=[VMEM((512, 512), BF16)], flops=2 * 64 * 512 * 512,
    )
    g0 = norms_part(0, store, s)
    g1 = norms_part(1, store, s)
    s1, s2, s3 = send(s1, dx=1), send(s2, dx=2), send(s3, dx=3)
    (h,) = call(round_sum, "round_sum", (s, s1, s2, s3, g0, g1), [piece], spaces={4: pl.ANY, 5: pl.ANY})
    o = send(h, dc=1)
    j1, j3, j2 = call(join, "join", (h, o), [shape((128, 512))] * 3)
    j = j1
    j1, j3, j2 = send(j1, dy=1), send(j3, dy=3), send(j2, dy=2)
    accs = [shape((4096, 128), F32)]
    work = 2 * 128 * 512 * 4096
    (acc,) = call(dots_first, "dots_first", (j, store), accs, flops=work)
    for d, got in ((1, j1), (3, j3)):
        (acc,) = call(
            lambda *f, d=d: dots_next(d, *f), "dots_next%d" % d, (got, store, acc), accs, flops=work, alias={2: 0},
        )
    norm = shape((32, 128), F32)
    own, gn, qn, z1, z2, z3 = call(
        lambda *f: dots_last(2, *f), "dots_last", (j2, j, j1, j3, store, acc, g0, g1),
        [shape((32, 4096), F32), norm, norm] + [shape((32, 4352))] * 3, flops=work,
    )
    z1, z2, z3 = send_layer(z1, 0), send_layer(z2, 1), send_layer(z3, 2)
    t, g, q = call(finish_first, "finish_first", (own, gn, qn, z1, z2), [shape((32, 4096), F32), norm, norm])
    out = pl.pallas_call(
        finish_last,
        name="finish_last",
        in_specs=[pl.BlockSpec(memory_space=VMEM)] * 4,
        out_specs=pl.BlockSpec(memory_space=pl.ANY),
        out_shape=shape((32, 4096), F32),
        scratch_shapes=[VMEM((32, 4096), F32), pltpu.SemaphoreType.DMA((4,))],
        compiler_params=pltpu.CompilerParams(vmem_limit_bytes=24 << 20),
    )(t, g, q, z3)
    return out.T


def solution(mesh):
    return jax.shard_map(
        shards,
        mesh=mesh,
        in_specs=(P("ex", "layer"), P("layer", "ex", None), P("ex", None, None, "layer"), P()),
        out_specs=P("ex", "layer"),
        check_vma=False,
    )
```

```python
import math

import jax
import jax.numpy as jnp
from jax import lax
from jax.experimental import pallas as pl
from jax.experimental.pallas import tpu as pltpu
from jax.sharding import PartitionSpec as P

BF16, F32 = jnp.bfloat16, jnp.float32
NT = (((1,), (1,)), ((), ()))
VMEM, HBM = pltpu.VMEM, pltpu.HBM
PART = 1024
PARTS = 4


def shape(dims, dtype=BF16):
    return jax.ShapeDtypeStruct(dims, dtype)


def place():
    e = lax.axis_index("ex")
    return e // 8, (e // 2) % 4, e % 2


def at(start, size):
    return pl.ds(pl.multiple_of(start, size), size)


def call(body, name, ins, outs, spaces=None, scratch=(), limit=24 << 20, flops=0, moved=1 << 20, alias=None):
    spaces = spaces or {}
    ins = [
        pltpu.with_memory_space_constraint(a, HBM) if spaces.get(i) is HBM else a
        for i, a in enumerate(ins)
    ]
    return pl.pallas_call(
        body,
        name=name,
        in_specs=[pl.BlockSpec(memory_space=spaces.get(i, VMEM)) for i in range(len(ins))],
        out_specs=[pl.BlockSpec(memory_space=VMEM)] * len(outs),
        out_shape=outs,
        scratch_shapes=scratch,
        input_output_aliases=alias or {},
        compiler_params=pltpu.CompilerParams(vmem_limit_bytes=limit),
        cost_estimate=pl.CostEstimate(flops=flops, bytes_accessed=moved, transcendentals=0),
    )(*ins)


def fetch(owners, q, p, w, qc, pv, o_ref, sems):
    x, y, c = place()
    copies = [
        pltpu.make_async_copy(owners, o_ref, sems.at[0]),
        pltpu.make_async_copy(q.at[at(c * 64, 64), :], qc, sems.at[1]),
        pltpu.make_async_copy(p, pv, sems.at[2]),
    ]
    for copy in copies:
        copy.start()
    copies[0].wait()
    o = o_ref[c]
    xback = lax.rem(x - o // 8 + 4, 4)
    yback = lax.rem(y - (o // 2) % 4 + 4, 4)
    tests = [o % 2 == c, o % 2 != c] + [xback == d for d in range(4)] + [yback == d for d in range(4)]
    for i, test in enumerate(tests):
        w[i, :, :] = jnp.full((64, 128), jnp.where(test, 1.0, 0.0), F32).astype(BF16)
    copies[1].wait()
    copies[2].wait()


def weigh(w, first, refs, columns):
    total = None
    for d, ref in enumerate(refs):
        term = ref(columns) * w[first + d, :, :]
        total = term if total is None else total + term
    return total


def slices(w, qc, qo, _, a0, a1, a2, a3):
    x, _, c = place()
    for d, a in enumerate((a0, a1, a2, a3)):
        for k in range(4):
            columns = at(lax.rem(x + d, 4) * 512 + 128 * k, 128)
            a[:, 128 * k:128 * k + 128] = weigh(
                w, 0, (lambda s: qc[:, s], lambda s: qo[at(c * 64, 64), s]), columns
            )


def cut(pv, _, b0, b1, b2, b3):
    _, y, _ = place()
    for d, b in enumerate((b0, b1, b2, b3)):
        b[...] = pv[:, at(lax.rem(y + d, 4) * 512, 512)]


def choose(w, a0, a1, a2, a3, r1, r2, r3):
    for k in range(4):
        columns = slice(128 * k, 128 * k + 128)
        got = weigh(w, 2, [lambda s, a=a: a[:, s] for a in (a0, a1, a2, a3)], columns)
        for r in (r1, r2, r3):
            r[:, columns] = got


def pick(w, r, u1, u2, u3, raw):
    for k in range(4):
        columns = slice(128 * k, 128 * k + 128)
        raw[:, columns] = weigh(w, 6, [lambda s, u=u: u[:, s] for u in (r, u1, u2, u3)], columns)


def product(raw, po, b0, b1, b2, b3, o1, o2, o3, s, s1, s2, s3, block):
    _, y, c = place()
    for d, (b, o) in enumerate(((b0, None), (b1, o1), (b2, o2), (b3, o3))):
        first = lax.rem(y - d + 4, 4) * 128
        block[at(first + c * 64, 64), :] = b[...]
        block[at(first + 64 - c * 64, 64), :] = po[:, at(y * 512, 512)] if o is None else o[...]
    total = jnp.dot(raw[...], block[...], preferred_element_type=F32)
    for ref in (s, s1, s2, s3):
        ref[...] = total


def round_sum(s0, s1, s2, s3, _, __, h):
    total = ((s0[...] + s2[...]) + (s1[...] + s3[...])).astype(BF16)
    h[...] = total * jnp.asarray(0.5, BF16)


WAYS = ((1, 3, 2), (2, 1, 3))


def slot(ahead, c):
    found = 0
    for k in range(3):
        found = jnp.where(ahead == jnp.where(c == 0, WAYS[0][k], WAYS[1][k]), k + 1, found)
    return found


def join(h, o, j1, j3, j2):
    _, _, c = place()
    layer = lax.axis_index("layer")
    for ref, block in ((h, c), (o, 1 - c)):
        for t in range(2):
            rows = at(slot(lax.rem(2 * block + t - layer + 4, 4), c) * 32, 32)
            for j in (j1, j3, j2):
                j[rows, :] = ref[32 * t:32 * t + 32, :]


def norms(part, v, after, gn):
    for i in range(8):
        rows = slice(2048 * part + 256 * i, 2048 * part + 256 * i + 256)
        squares = None
        for k in range(16):
            t = v[rows, 128 * k:128 * k + 128].astype(F32)
            squares = t * t if squares is None else squares + t * t
        line = jnp.sum(squares.T, axis=0, keepdims=True) * 0.5
        for k in range(2):
            gn[2 * i + k:2 * i + k + 1, :] = line[:, 128 * k:128 * k + 128]


def term(d, j, v, rows):
    _, y, _ = place()
    columns = at(lax.rem(y - d + 4, 4) * 512, 512)
    return lax.dot_general(v[rows, columns], j[...], NT, preferred_element_type=F32)


def dots_first(j, v, acc):
    for i in range(PARTS):
        rows = slice(PART * i, PART * i + PART)
        acc[rows, :] = term(0, j, v, rows)


def dots_next(d, j, v, old, acc):
    for i in range(PARTS):
        rows = slice(PART * i, PART * i + PART)
        acc[rows, :] = old[rows, :] + term(d, j, v, rows)


def dots_last(d, j, j0, ja, jb, v, old, g0, g1, own, gn, qn, z1, z2, z3):
    zs = ((1, z1), (2, z2), (3, z3))
    for i in range(PARTS):
        rows = slice(PART * i, PART * i + PART)
        out = (old[rows, :] + term(d, j, v, rows)).T
        own[:, rows] = out[0:32, :]
        for e, z in zs:
            z[:, rows] = out[32 * e:32 * e + 32, :].astype(BF16)
    total = None
    for piece in (j, j0, ja, jb):
        for k in range(4):
            t = piece[:, 128 * k:128 * k + 128].astype(F32)
            total = t * t if total is None else total + t * t
    qsum = jnp.broadcast_to(jnp.sum(total, axis=1, keepdims=True), (128, 128))
    qn[...] = qsum[0:32, :]
    for i, g in enumerate((g0, g1)):
        gn[16 * i:16 * i + 16, :] = g[...]
    lane = lax.broadcasted_iota(jnp.int32, (32, 128), 1)
    for e, z in zs:
        part = qsum[32 * e:32 * e + 32, :]
        top = part.astype(BF16).astype(F32)
        z[:, 4096:4224] = gn[...].astype(BF16)
        z[:, 4224:4352] = jnp.where(lane < 64, top, part - top).astype(BF16)


def norm_parts(z):
    return z[:, 4096:4224].astype(F32), z[:, 4224:4225].astype(F32) + z[:, 4288:4289].astype(F32)


def finish_first(own, gn, qn, z1, z3, t, g, q):
    g1, q1 = norm_parts(z1)
    g3, q3 = norm_parts(z3)
    g[...] = gn[...] + (g1 + g3)
    q[...] = jnp.broadcast_to(qn[:, 0:1] + (q1 + q3), (32, 128))
    for i in range(32):
        columns = slice(128 * i, 128 * i + 128)
        t[:, columns] = own[:, columns] + (z1[:, columns].astype(F32) + z3[:, columns].astype(F32))


def finish_last(t, g, q, z2, out, part, sems):
    g2, q2 = norm_parts(z2)
    g = lax.rsqrt((g[...] + g2) * 2.0 + 1e-06)
    q = lax.rsqrt((q[:, 0:1] + q2) * 4.0 + 1e-06) * (2.0 * math.sqrt(8192.0))
    copies = []
    for n in range(4):
        for i in range(8 * n, 8 * n + 8):
            columns = slice(128 * i, 128 * i + 128)
            part[:, columns] = (t[:, columns] + z2[:, columns].astype(F32)) * g[i:i + 1, :] * q
        columns = pl.ds(1024 * n, 1024)
        copies.append(pltpu.make_async_copy(part.at[:, columns], out.at[:, columns], sems.at[n]))
        copies[-1].start()
    for copy in copies:
        copy.wait()


def moved(dx, dy, dc):
    pairs = []
    for x in range(4):
        for y in range(4):
            for c in range(2):
                to = ((x + dx) % 4 * 4 + (y + dy) % 4) * 2 + (c + dc) % 2
                pairs.append(((x * 4 + y) * 2 + c, to))
    return pairs


def send(a, dx=0, dy=0, dc=0):
    return lax.ppermute(a, "ex", moved(dx, dy, dc))


def send_layer(a, k):
    pairs = []
    for e in range(32):
        for layer in range(4):
            pairs.append((4 * e + layer, 4 * e + (layer + WAYS[e % 2][k]) % 4))
    return lax.ppermute(a, ("ex", "layer"), pairs)


def norms_part(part, store, after):
    return call(
        lambda *refs: norms(part, *refs), "norms%d" % part, (store, after), [shape((16, 128), F32)],
        spaces={1: pl.ANY}, flops=3 * 2048 * 2048, moved=8 << 20,
    )[0]


def shards(store, precond, query_slots, owners):
    q = query_slots.reshape(128, 2048)
    p = precond.reshape(64, 2048)
    qo = send(q, dc=1)
    po = send(p, dc=1)
    piece = shape((64, 512))
    w, qc, pv = call(
        fetch, "fetch", (owners, q, p), [shape((10, 64, 128)), shape((64, 2048)), shape((64, 2048))],
        spaces={0: HBM, 1: HBM, 2: HBM}, scratch=[pltpu.SMEM((2,), jnp.int32), pltpu.SemaphoreType.DMA((3,))],
    )
    a0, a1, a2, a3 = call(slices, "slices", (w, qc, qo, store), [piece] * 4, spaces={3: HBM})
    a1, a2, a3 = send(a1, dx=1), send(a2, dx=2), send(a3, dx=3)
    b0, b1, b2, b3 = call(cut, "cut", (pv, a0), [piece] * 4, spaces={1: pl.ANY})
    b1, b2, b3 = send(b1, dy=1), send(b2, dy=2), send(b3, dy=3)
    r1, r2, r3 = call(choose, "choose", (w, a0, a1, a2, a3), [piece] * 3)
    r = r1
    r1, r2, r3 = send(r1, dy=1), send(r2, dy=2), send(r3, dy=3)
    o1, o2, o3 = send(b1, dc=1), send(b2, dc=1), send(b3, dc=1)
    (raw,) = call(pick, "pick", (w, r, r1, r2, r3), [piece])
    s, s1, s2, s3 = call(
        product, "product", (raw, po, b0, b1, b2, b3, o1, o2, o3), [shape((64, 512), F32)] * 4,
        scratch=[VMEM((512, 512), BF16)], flops=2 * 64 * 512 * 512,
    )
    g0 = norms_part(0, store, s)
    g1 = norms_part(1, store, s)
    s1, s2, s3 = send(s1, dx=1), send(s2, dx=2), send(s3, dx=3)
    (h,) = call(round_sum, "round_sum", (s, s1, s2, s3, g0, g1), [piece], spaces={4: pl.ANY, 5: pl.ANY})
    o = send(h, dc=1)
    j1, j3, j2 = call(join, "join", (h, o), [shape((128, 512))] * 3)
    j = j1
    j1, j3, j2 = send(j1, dy=1), send(j3, dy=3), send(j2, dy=2)
    accs = [shape((4096, 128), F32)]
    work = 2 * 128 * 512 * 4096
    (acc,) = call(dots_first, "dots_first", (j, store), accs, flops=work)
    for d, got in ((1, j1), (3, j3)):
        (acc,) = call(
            lambda *f, d=d: dots_next(d, *f), "dots_next%d" % d, (got, store, acc), accs, flops=work, alias={2: 0},
        )
    norm = shape((32, 128), F32)
    own, gn, qn, z1, z2, z3 = call(
        lambda *f: dots_last(2, *f), "dots_last", (j2, j, j1, j3, store, acc, g0, g1),
        [shape((32, 4096), F32), norm, norm] + [shape((32, 4352))] * 3, flops=work,
    )
    z1, z2, z3 = send_layer(z1, 0), send_layer(z2, 1), send_layer(z3, 2)
    t, g, q = call(finish_first, "finish_first", (own, gn, qn, z1, z2), [shape((32, 4096), F32), norm, norm])
    out = pl.pallas_call(
        finish_last,
        name="finish_last",
        in_specs=[pl.BlockSpec(memory_space=VMEM)] * 4,
        out_specs=pl.BlockSpec(memory_space=pl.ANY),
        out_shape=shape((32, 4096), F32),
        scratch_shapes=[VMEM((32, 4096), F32), pltpu.SemaphoreType.DMA((4,))],
        compiler_params=pltpu.CompilerParams(vmem_limit_bytes=24 << 20),
    )(t, g, q, z3)
    return out.T


def solution(mesh):
    return jax.shard_map(
        shards,
        mesh=mesh,
        in_specs=(P("ex", "layer"), P("layer", "ex", None), P("ex", None, None, "layer"), P()),
        out_specs=P("ex", "layer"),
        check_vma=False,
    )
```

```python
import math

import jax
import jax.numpy as jnp
from jax import lax
from jax.experimental import pallas as pl
from jax.experimental.pallas import tpu as pltpu
from jax.sharding import PartitionSpec as P

BF16, F32 = jnp.bfloat16, jnp.float32
NT = (((1,), (1,)), ((), ()))
VMEM, HBM = pltpu.VMEM, pltpu.HBM
PART = 1024
PARTS = 4


def shape(dims, dtype=BF16):
    return jax.ShapeDtypeStruct(dims, dtype)


def place():
    e = lax.axis_index("ex")
    return e // 8, (e // 2) % 4, e % 2


def at(start, size):
    return pl.ds(pl.multiple_of(start, size), size)


def call(body, name, ins, outs, spaces=None, scratch=(), limit=24 << 20, flops=0, moved=1 << 20, alias=None):
    spaces = spaces or {}
    ins = [
        pltpu.with_memory_space_constraint(a, HBM) if spaces.get(i) is HBM else a
        for i, a in enumerate(ins)
    ]
    return pl.pallas_call(
        body,
        name=name,
        in_specs=[pl.BlockSpec(memory_space=spaces.get(i, VMEM)) for i in range(len(ins))],
        out_specs=[pl.BlockSpec(memory_space=VMEM)] * len(outs),
        out_shape=outs,
        scratch_shapes=scratch,
        input_output_aliases=alias or {},
        compiler_params=pltpu.CompilerParams(vmem_limit_bytes=limit),
        cost_estimate=pl.CostEstimate(flops=flops, bytes_accessed=moved, transcendentals=0),
    )(*ins)


def fetch(owners, q, p, w, qc, pv, o_ref, sems):
    x, y, c = place()
    copies = [
        pltpu.make_async_copy(owners, o_ref, sems.at[0]),
        pltpu.make_async_copy(q.at[at(c * 64, 64), :], qc, sems.at[1]),
        pltpu.make_async_copy(p, pv, sems.at[2]),
    ]
    for copy in copies:
        copy.start()
    copies[0].wait()
    o = o_ref[c]
    xback = lax.rem(x - o // 8 + 4, 4)
    yback = lax.rem(y - (o // 2) % 4 + 4, 4)
    tests = [o % 2 == c, o % 2 != c] + [xback == d for d in range(4)] + [yback == d for d in range(4)]
    for i, test in enumerate(tests):
        w[i, :, :] = jnp.full((64, 128), jnp.where(test, 1.0, 0.0), F32).astype(BF16)
    copies[1].wait()
    copies[2].wait()


def weigh(w, first, refs, columns):
    total = None
    for d, ref in enumerate(refs):
        term = ref(columns) * w[first + d, :, :]
        total = term if total is None else total + term
    return total


def slices(w, qc, qo, _, a0, a1, a2, a3):
    x, _, c = place()
    for d, a in enumerate((a0, a1, a2, a3)):
        for k in range(4):
            columns = at(lax.rem(x + d, 4) * 512 + 128 * k, 128)
            a[:, 128 * k:128 * k + 128] = weigh(
                w, 0, (lambda s: qc[:, s], lambda s: qo[at(c * 64, 64), s]), columns
            )


def cut(pv, _, b0, b1, b2, b3):
    _, y, _ = place()
    for d, b in enumerate((b0, b1, b2, b3)):
        b[...] = pv[:, at(lax.rem(y + d, 4) * 512, 512)]


def choose(w, a0, a1, a2, a3, r1, r2, r3):
    for k in range(4):
        columns = slice(128 * k, 128 * k + 128)
        got = weigh(w, 2, [lambda s, a=a: a[:, s] for a in (a0, a1, a2, a3)], columns)
        for r in (r1, r2, r3):
            r[:, columns] = got


def pick(w, r, u1, u2, u3, raw):
    for k in range(4):
        columns = slice(128 * k, 128 * k + 128)
        raw[:, columns] = weigh(w, 6, [lambda s, u=u: u[:, s] for u in (r, u1, u2, u3)], columns)


def product(raw, po, b0, b1, b2, b3, o1, o2, o3, s, s1, s2, s3, block):
    _, y, c = place()
    for d, (b, o) in enumerate(((b0, None), (b1, o1), (b2, o2), (b3, o3))):
        first = lax.rem(y - d + 4, 4) * 128
        block[at(first + c * 64, 64), :] = b[...]
        block[at(first + 64 - c * 64, 64), :] = po[:, at(y * 512, 512)] if o is None else o[...]
    total = jnp.dot(raw[...], block[...], preferred_element_type=F32)
    for ref in (s, s1, s2, s3):
        ref[...] = total


def round_sum(s0, s1, s2, s3, _, __, h):
    total = ((s0[...] + s2[...]) + (s1[...] + s3[...])).astype(BF16)
    h[...] = total * jnp.asarray(0.5, BF16)


WAYS = ((1, 3, 2), (2, 1, 3))


def slot(ahead, c):
    found = 0
    for k in range(3):
        found = jnp.where(ahead == jnp.where(c == 0, WAYS[0][k], WAYS[1][k]), k + 1, found)
    return found


def join(h, o, j1, j3, j2):
    _, _, c = place()
    layer = lax.axis_index("layer")
    for ref, block in ((h, c), (o, 1 - c)):
        for t in range(2):
            rows = at(slot(lax.rem(2 * block + t - layer + 4, 4), c) * 32, 32)
            for j in (j1, j3, j2):
                j[rows, :] = ref[32 * t:32 * t + 32, :]


def norms(part, v, after, gn):
    for i in range(8):
        rows = slice(2048 * part + 256 * i, 2048 * part + 256 * i + 256)
        squares = None
        for k in range(16):
            t = v[rows, 128 * k:128 * k + 128].astype(F32)
            squares = t * t if squares is None else squares + t * t
        line = jnp.sum(squares.T, axis=0, keepdims=True) * 0.5
        for k in range(2):
            gn[2 * i + k:2 * i + k + 1, :] = line[:, 128 * k:128 * k + 128]


def term(d, j, v, rows):
    _, y, _ = place()
    columns = at(lax.rem(y - d + 4, 4) * 512, 512)
    return lax.dot_general(v[rows, columns], j[...], NT, preferred_element_type=F32)


def dots_first(j, v, acc):
    for i in range(PARTS):
        rows = slice(PART * i, PART * i + PART)
        acc[rows, :] = term(0, j, v, rows)


def dots_next(d, j, v, old, acc):
    for i in range(PARTS):
        rows = slice(PART * i, PART * i + PART)
        acc[rows, :] = old[rows, :] + term(d, j, v, rows)


def squares(pieces):
    total = None
    for piece in pieces:
        for k in range(4):
            t = piece[:, 128 * k:128 * k + 128].astype(F32)
            total = t * t if total is None else total + t * t
    return total


def dots_third(d, j, j0, ja, v, old, acc, sq):
    dots_next(d, j, v, old, acc)
    sq[...] = squares((j, j0, ja))


def dots_last(d, j, sq, v, old, g0, g1, own, gn, qn, z1, z2, z3):
    zs = ((1, z1), (2, z2), (3, z3))
    for i in range(PARTS):
        rows = slice(PART * i, PART * i + PART)
        out = (old[rows, :] + term(d, j, v, rows)).T
        own[:, rows] = out[0:32, :]
        for e, z in zs:
            z[:, rows] = out[32 * e:32 * e + 32, :].astype(BF16)
    total = sq[...] + squares((j,))
    qsum = jnp.broadcast_to(jnp.sum(total, axis=1, keepdims=True), (128, 128))
    qn[...] = qsum[0:32, :]
    for i, g in enumerate((g0, g1)):
        gn[16 * i:16 * i + 16, :] = g[...]
    lane = lax.broadcasted_iota(jnp.int32, (32, 128), 1)
    for e, z in zs:
        part = qsum[32 * e:32 * e + 32, :]
        top = part.astype(BF16).astype(F32)
        z[:, 4096:4224] = gn[...].astype(BF16)
        z[:, 4224:4352] = jnp.where(lane < 64, top, part - top).astype(BF16)


def norm_parts(z):
    return z[:, 4096:4224].astype(F32), z[:, 4224:4225].astype(F32) + z[:, 4288:4289].astype(F32)


def finish_first(own, gn, qn, z1, z3, t, g, q):
    g1, q1 = norm_parts(z1)
    g3, q3 = norm_parts(z3)
    g[...] = gn[...] + (g1 + g3)
    q[...] = jnp.broadcast_to(qn[:, 0:1] + (q1 + q3), (32, 128))
    for i in range(32):
        columns = slice(128 * i, 128 * i + 128)
        t[:, columns] = own[:, columns] + (z1[:, columns].astype(F32) + z3[:, columns].astype(F32))


def finish_last(t, g, q, z2, out, part, sems):
    g2, q2 = norm_parts(z2)
    g = lax.rsqrt((g[...] + g2) * 2.0 + 1e-06)
    q = lax.rsqrt((q[:, 0:1] + q2) * 4.0 + 1e-06) * (2.0 * math.sqrt(8192.0))
    copies = []
    for n in range(4):
        for i in range(8 * n, 8 * n + 8):
            columns = slice(128 * i, 128 * i + 128)
            part[:, columns] = (t[:, columns] + z2[:, columns].astype(F32)) * g[i:i + 1, :] * q
        columns = pl.ds(1024 * n, 1024)
        copies.append(pltpu.make_async_copy(part.at[:, columns], out.at[:, columns], sems.at[n]))
        copies[-1].start()
    for copy in copies:
        copy.wait()


def moved(dx, dy, dc):
    pairs = []
    for x in range(4):
        for y in range(4):
            for c in range(2):
                to = ((x + dx) % 4 * 4 + (y + dy) % 4) * 2 + (c + dc) % 2
                pairs.append(((x * 4 + y) * 2 + c, to))
    return pairs


def send(a, dx=0, dy=0, dc=0):
    return lax.ppermute(a, "ex", moved(dx, dy, dc))


def send_layer(a, k):
    pairs = []
    for e in range(32):
        for layer in range(4):
            pairs.append((4 * e + layer, 4 * e + (layer + WAYS[e % 2][k]) % 4))
    return lax.ppermute(a, ("ex", "layer"), pairs)


def norms_part(part, store, after):
    return call(
        lambda *refs: norms(part, *refs), "norms%d" % part, (store, after), [shape((16, 128), F32)],
        spaces={1: pl.ANY}, flops=3 * 2048 * 2048, moved=8 << 20,
    )[0]


def shards(store, precond, query_slots, owners):
    q = query_slots.reshape(128, 2048)
    p = precond.reshape(64, 2048)
    qo = send(q, dc=1)
    po = send(p, dc=1)
    piece = shape((64, 512))
    w, qc, pv = call(
        fetch, "fetch", (owners, q, p), [shape((10, 64, 128)), shape((64, 2048)), shape((64, 2048))],
        spaces={0: HBM, 1: HBM, 2: HBM}, scratch=[pltpu.SMEM((2,), jnp.int32), pltpu.SemaphoreType.DMA((3,))],
    )
    a0, a1, a2, a3 = call(slices, "slices", (w, qc, qo, store), [piece] * 4, spaces={3: HBM})
    a1, a2, a3 = send(a1, dx=1), send(a2, dx=2), send(a3, dx=3)
    b0, b1, b2, b3 = call(cut, "cut", (pv, a0), [piece] * 4, spaces={1: pl.ANY})
    b1, b2, b3 = send(b1, dy=1), send(b2, dy=2), send(b3, dy=3)
    r1, r2, r3 = call(choose, "choose", (w, a0, a1, a2, a3), [piece] * 3)
    r = r1
    r1, r2, r3 = send(r1, dy=1), send(r2, dy=2), send(r3, dy=3)
    o1, o2, o3 = send(b1, dc=1), send(b2, dc=1), send(b3, dc=1)
    (raw,) = call(pick, "pick", (w, r, r1, r2, r3), [piece])
    s, s1, s2, s3 = call(
        product, "product", (raw, po, b0, b1, b2, b3, o1, o2, o3), [shape((64, 512), F32)] * 4,
        scratch=[VMEM((512, 512), BF16)], flops=2 * 64 * 512 * 512,
    )
    g0 = norms_part(0, store, s)
    g1 = norms_part(1, store, s)
    s1, s2, s3 = send(s1, dx=1), send(s2, dx=2), send(s3, dx=3)
    (h,) = call(round_sum, "round_sum", (s, s1, s2, s3, g0, g1), [piece], spaces={4: pl.ANY, 5: pl.ANY})
    o = send(h, dc=1)
    j1, j3, j2 = call(join, "join", (h, o), [shape((128, 512))] * 3)
    j = j1
    j1, j3, j2 = send(j1, dy=1), send(j3, dy=3), send(j2, dy=2)
    accs = [shape((4096, 128), F32)]
    work = 2 * 128 * 512 * 4096
    (acc,) = call(dots_first, "dots_first", (j, store), accs, flops=work)
    (acc,) = call(
        lambda *f: dots_next(1, *f), "dots_next1", (j1, store, acc), accs, flops=work, alias={2: 0},
    )
    acc, sq = call(
        lambda *f: dots_third(3, *f), "dots_next3", (j3, j, j1, store, acc), accs + [shape((128, 128), F32)],
        flops=work, alias={4: 0},
    )
    norm = shape((32, 128), F32)
    own, gn, qn, z1, z2, z3 = call(
        lambda *f: dots_last(2, *f), "dots_last", (j2, sq, store, acc, g0, g1),
        [shape((32, 4096), F32), norm, norm] + [shape((32, 4352))] * 3, flops=work,
    )
    z1, z2, z3 = send_layer(z1, 0), send_layer(z2, 1), send_layer(z3, 2)
    t, g, q = call(finish_first, "finish_first", (own, gn, qn, z1, z2), [shape((32, 4096), F32), norm, norm])
    out = pl.pallas_call(
        finish_last,
        name="finish_last",
        in_specs=[pl.BlockSpec(memory_space=VMEM)] * 4,
        out_specs=pl.BlockSpec(memory_space=pl.ANY),
        out_shape=shape((32, 4096), F32),
        scratch_shapes=[VMEM((32, 4096), F32), pltpu.SemaphoreType.DMA((4,))],
        compiler_params=pltpu.CompilerParams(vmem_limit_bytes=24 << 20),
    )(t, g, q, z3)
    return out.T


def solution(mesh):
    return jax.shard_map(
        shards,
        mesh=mesh,
        in_specs=(P("ex", "layer"), P("layer", "ex", None), P("ex", None, None, "layer"), P()),
        out_specs=P("ex", "layer"),
        check_vma=False,
    )
```

```python
import math

import jax
import jax.numpy as jnp
from jax import lax
from jax.experimental import pallas as pl
from jax.experimental.pallas import tpu as pltpu
from jax.sharding import PartitionSpec as P

BF16, F32 = jnp.bfloat16, jnp.float32
NT = (((1,), (1,)), ((), ()))
VMEM, HBM = pltpu.VMEM, pltpu.HBM
PART = 1024
PARTS = 4


def shape(dims, dtype=BF16):
    return jax.ShapeDtypeStruct(dims, dtype)


def place():
    e = lax.axis_index("ex")
    return e // 8, (e // 2) % 4, e % 2


def at(start, size):
    return pl.ds(pl.multiple_of(start, size), size)


def call(body, name, ins, outs, spaces=None, scratch=(), limit=24 << 20, flops=0, moved=1 << 20, alias=None):
    spaces = spaces or {}
    ins = [
        pltpu.with_memory_space_constraint(a, HBM) if spaces.get(i) is HBM else a
        for i, a in enumerate(ins)
    ]
    return pl.pallas_call(
        body,
        name=name,
        in_specs=[pl.BlockSpec(memory_space=spaces.get(i, VMEM)) for i in range(len(ins))],
        out_specs=[pl.BlockSpec(memory_space=VMEM)] * len(outs),
        out_shape=outs,
        scratch_shapes=scratch,
        input_output_aliases=alias or {},
        compiler_params=pltpu.CompilerParams(vmem_limit_bytes=limit),
        cost_estimate=pl.CostEstimate(flops=flops, bytes_accessed=moved, transcendentals=0),
    )(*ins)


def fetch(owners, q, p, w, qc, pv, o_ref, sems):
    x, y, c = place()
    copies = [
        pltpu.make_async_copy(owners, o_ref, sems.at[0]),
        pltpu.make_async_copy(q.at[at(c * 64, 64), :], qc, sems.at[1]),
        pltpu.make_async_copy(p, pv, sems.at[2]),
    ]
    for copy in copies:
        copy.start()
    copies[0].wait()
    o = o_ref[c]
    xback = lax.rem(x - o // 8 + 4, 4)
    yback = lax.rem(y - (o // 2) % 4 + 4, 4)
    tests = [o % 2 == c, o % 2 != c] + [xback == d for d in range(4)] + [yback == d for d in range(4)]
    for i, test in enumerate(tests):
        w[i, :, :] = jnp.full((64, 128), jnp.where(test, 1.0, 0.0), F32).astype(BF16)
    copies[1].wait()
    copies[2].wait()


def weigh(w, first, refs, columns):
    total = None
    for d, ref in enumerate(refs):
        term = ref(columns) * w[first + d, :, :]
        total = term if total is None else total + term
    return total


def slices(w, qc, qo, _, a0, a1, a2, a3):
    x, _, c = place()
    for d, a in enumerate((a0, a1, a2, a3)):
        for k in range(4):
            columns = at(lax.rem(x + d, 4) * 512 + 128 * k, 128)
            a[:, 128 * k:128 * k + 128] = weigh(
                w, 0, (lambda s: qc[:, s], lambda s: qo[at(c * 64, 64), s]), columns
            )


def cut(pv, _, b0, b1, b2, b3):
    _, y, _ = place()
    for d, b in enumerate((b0, b1, b2, b3)):
        b[...] = pv[:, at(lax.rem(y + d, 4) * 512, 512)]


def choose(w, a0, a1, a2, a3, r1, r2, r3):
    for k in range(4):
        columns = slice(128 * k, 128 * k + 128)
        got = weigh(w, 2, [lambda s, a=a: a[:, s] for a in (a0, a1, a2, a3)], columns)
        for r in (r1, r2, r3):
            r[:, columns] = got


def pick(w, r, u1, u2, u3, raw):
    for k in range(4):
        columns = slice(128 * k, 128 * k + 128)
        raw[:, columns] = weigh(w, 6, [lambda s, u=u: u[:, s] for u in (r, u1, u2, u3)], columns)


def product(raw, po, b0, b1, b2, b3, o1, o2, o3, s, s1, s2, s3, block):
    _, y, c = place()
    for d, (b, o) in enumerate(((b0, None), (b1, o1), (b2, o2), (b3, o3))):
        first = lax.rem(y - d + 4, 4) * 128
        block[at(first + c * 64, 64), :] = b[...]
        block[at(first + 64 - c * 64, 64), :] = po[:, at(y * 512, 512)] if o is None else o[...]
    total = jnp.dot(raw[...], block[...], preferred_element_type=F32)
    for ref in (s, s1, s2, s3):
        ref[...] = total


def round_sum(s0, s1, s2, s3, _, __, h):
    total = ((s0[...] + s2[...]) + (s1[...] + s3[...])).astype(BF16)
    h[...] = total * jnp.asarray(0.5, BF16)


WAYS = ((1, 3, 2), (2, 3, 1))


def slot(ahead, c):
    found = 0
    for k in range(3):
        found = jnp.where(ahead == jnp.where(c == 0, WAYS[0][k], WAYS[1][k]), k + 1, found)
    return found


def join(h, o, j1, j3, j2):
    _, _, c = place()
    layer = lax.axis_index("layer")
    for ref, block in ((h, c), (o, 1 - c)):
        for t in range(2):
            rows = at(slot(lax.rem(2 * block + t - layer + 4, 4), c) * 32, 32)
            for j in (j1, j3, j2):
                j[rows, :] = ref[32 * t:32 * t + 32, :]


def norms(part, v, after, gn):
    for i in range(8):
        rows = slice(2048 * part + 256 * i, 2048 * part + 256 * i + 256)
        squares = None
        for k in range(16):
            t = v[rows, 128 * k:128 * k + 128].astype(F32)
            squares = t * t if squares is None else squares + t * t
        line = jnp.sum(squares.T, axis=0, keepdims=True) * 0.5
        for k in range(2):
            gn[2 * i + k:2 * i + k + 1, :] = line[:, 128 * k:128 * k + 128]


def term(d, j, v, rows):
    _, y, _ = place()
    columns = at(lax.rem(y - d + 4, 4) * 512, 512)
    return lax.dot_general(v[rows, columns], j[...], NT, preferred_element_type=F32)


def dots_first(j, v, acc):
    for i in range(PARTS):
        rows = slice(PART * i, PART * i + PART)
        acc[rows, :] = term(0, j, v, rows)


def dots_next(d, j, v, old, acc):
    for i in range(PARTS):
        rows = slice(PART * i, PART * i + PART)
        acc[rows, :] = old[rows, :] + term(d, j, v, rows)


def dots_last(d, j, j0, ja, jb, v, old, g0, g1, own, gn, qn, z1, z2, z3):
    zs = ((1, z1), (2, z2), (3, z3))
    for i in range(PARTS):
        rows = slice(PART * i, PART * i + PART)
        out = (old[rows, :] + term(d, j, v, rows)).T
        own[:, rows] = out[0:32, :]
        for e, z in zs:
            z[:, rows] = out[32 * e:32 * e + 32, :].astype(BF16)
    total = None
    for piece in (j, j0, ja, jb):
        for k in range(4):
            t = piece[:, 128 * k:128 * k + 128].astype(F32)
            total = t * t if total is None else total + t * t
    qsum = jnp.broadcast_to(jnp.sum(total, axis=1, keepdims=True), (128, 128))
    qn[...] = qsum[0:32, :]
    for i, g in enumerate((g0, g1)):
        gn[16 * i:16 * i + 16, :] = g[...]
    lane = lax.broadcasted_iota(jnp.int32, (32, 128), 1)
    for e, z in zs:
        part = qsum[32 * e:32 * e + 32, :]
        top = part.astype(BF16).astype(F32)
        z[:, 4096:4224] = gn[...].astype(BF16)
        z[:, 4224:4352] = jnp.where(lane < 64, top, part - top).astype(BF16)


def norm_parts(z):
    return z[:, 4096:4224].astype(F32), z[:, 4224:4225].astype(F32) + z[:, 4288:4289].astype(F32)


def finish_first(own, gn, qn, z1, z3, t, g, q):
    g1, q1 = norm_parts(z1)
    g3, q3 = norm_parts(z3)
    g[...] = gn[...] + (g1 + g3)
    q[...] = jnp.broadcast_to(qn[:, 0:1] + (q1 + q3), (32, 128))
    for i in range(32):
        columns = slice(128 * i, 128 * i + 128)
        t[:, columns] = own[:, columns] + (z1[:, columns].astype(F32) + z3[:, columns].astype(F32))


def finish_last(t, g, q, z2, out, part, sems):
    g2, q2 = norm_parts(z2)
    g = lax.rsqrt((g[...] + g2) * 2.0 + 1e-06)
    q = lax.rsqrt((q[:, 0:1] + q2) * 4.0 + 1e-06) * (2.0 * math.sqrt(8192.0))
    copies = []
    for n in range(4):
        for i in range(8 * n, 8 * n + 8):
            columns = slice(128 * i, 128 * i + 128)
            part[:, columns] = (t[:, columns] + z2[:, columns].astype(F32)) * g[i:i + 1, :] * q
        columns = pl.ds(1024 * n, 1024)
        copies.append(pltpu.make_async_copy(part.at[:, columns], out.at[:, columns], sems.at[n]))
        copies[-1].start()
    for copy in copies:
        copy.wait()


def moved(dx, dy, dc):
    pairs = []
    for x in range(4):
        for y in range(4):
            for c in range(2):
                to = ((x + dx) % 4 * 4 + (y + dy) % 4) * 2 + (c + dc) % 2
                pairs.append(((x * 4 + y) * 2 + c, to))
    return pairs


def send(a, dx=0, dy=0, dc=0):
    return lax.ppermute(a, "ex", moved(dx, dy, dc))


def send_layer(a, k):
    pairs = []
    for e in range(32):
        for layer in range(4):
            pairs.append((4 * e + layer, 4 * e + (layer + WAYS[e % 2][k]) % 4))
    return lax.ppermute(a, ("ex", "layer"), pairs)


def norms_part(part, store, after):
    return call(
        lambda *refs: norms(part, *refs), "norms%d" % part, (store, after), [shape((16, 128), F32)],
        spaces={1: pl.ANY}, flops=3 * 2048 * 2048, moved=8 << 20,
    )[0]


def shards(store, precond, query_slots, owners):
    q = query_slots.reshape(128, 2048)
    p = precond.reshape(64, 2048)
    qo = send(q, dc=1)
    po = send(p, dc=1)
    piece = shape((64, 512))
    w, qc, pv = call(
        fetch, "fetch", (owners, q, p), [shape((10, 64, 128)), shape((64, 2048)), shape((64, 2048))],
        spaces={0: HBM, 1: HBM, 2: HBM}, scratch=[pltpu.SMEM((2,), jnp.int32), pltpu.SemaphoreType.DMA((3,))],
    )
    a0, a1, a2, a3 = call(slices, "slices", (w, qc, qo, store), [piece] * 4, spaces={3: HBM})
    a1, a2, a3 = send(a1, dx=1), send(a2, dx=2), send(a3, dx=3)
    b0, b1, b2, b3 = call(cut, "cut", (pv, a0), [piece] * 4, spaces={1: pl.ANY})
    b1, b2, b3 = send(b1, dy=1), send(b2, dy=2), send(b3, dy=3)
    r1, r2, r3 = call(choose, "choose", (w, a0, a1, a2, a3), [piece] * 3)
    r = r1
    r1, r2, r3 = send(r1, dy=1), send(r2, dy=2), send(r3, dy=3)
    o1, o2, o3 = send(b1, dc=1), send(b2, dc=1), send(b3, dc=1)
    (raw,) = call(pick, "pick", (w, r, r1, r2, r3), [piece])
    s, s1, s2, s3 = call(
        product, "product", (raw, po, b0, b1, b2, b3, o1, o2, o3), [shape((64, 512), F32)] * 4,
        scratch=[VMEM((512, 512), BF16)], flops=2 * 64 * 512 * 512,
    )
    g0 = norms_part(0, store, s)
    g1 = norms_part(1, store, s)
    s1, s2, s3 = send(s1, dx=1), send(s2, dx=2), send(s3, dx=3)
    (h,) = call(round_sum, "round_sum", (s, s1, s2, s3, g0, g1), [piece], spaces={4: pl.ANY, 5: pl.ANY})
    o = send(h, dc=1)
    j1, j3, j2 = call(join, "join", (h, o), [shape((128, 512))] * 3)
    j = j1
    j1, j3, j2 = send(j1, dy=1), send(j3, dy=3), send(j2, dy=2)
    accs = [shape((4096, 128), F32)]
    work = 2 * 128 * 512 * 4096
    (acc,) = call(dots_first, "dots_first", (j, store), accs, flops=work)
    for d, got in ((1, j1), (3, j3)):
        (acc,) = call(
            lambda *f, d=d: dots_next(d, *f), "dots_next%d" % d, (got, store, acc), accs, flops=work, alias={2: 0},
        )
    norm = shape((32, 128), F32)
    own, gn, qn, z1, z2, z3 = call(
        lambda *f: dots_last(2, *f), "dots_last", (j2, j, j1, j3, store, acc, g0, g1),
        [shape((32, 4096), F32), norm, norm] + [shape((32, 4352))] * 3, flops=work,
    )
    z1, z2, z3 = send_layer(z1, 0), send_layer(z2, 1), send_layer(z3, 2)
    t, g, q = call(finish_first, "finish_first", (own, gn, qn, z1, z2), [shape((32, 4096), F32), norm, norm])
    out = pl.pallas_call(
        finish_last,
        name="finish_last",
        in_specs=[pl.BlockSpec(memory_space=VMEM)] * 4,
        out_specs=pl.BlockSpec(memory_space=pl.ANY),
        out_shape=shape((32, 4096), F32),
        scratch_shapes=[VMEM((32, 4096), F32), pltpu.SemaphoreType.DMA((4,))],
        compiler_params=pltpu.CompilerParams(vmem_limit_bytes=24 << 20),
    )(t, g, q, z3)
    return out.T


def solution(mesh):
    return jax.shard_map(
        shards,
        mesh=mesh,
        in_specs=(P("ex", "layer"), P("layer", "ex", None), P("ex", None, None, "layer"), P()),
        out_specs=P("ex", "layer"),
        check_vma=False,
    )
```
